32 devices in a mesh: row: 8 (over z, core), col: 4 (over y, x).
Axes of the slice: x: 2, y: 2, z: 4, core: 2. Of those that a mesh axis runs over, the one named last changes fastest.
Arguments:
- covariance: float32 [8192, 8192], P('row', 'col')
- lon_speed: float32 [8192], replicated, may hold values from 0.05 to 0.45
- lat_speed: float32 [8192], replicated, may hold values from 0.05 to 0.45
- lon_sign: int32 [8192], replicated, may hold values from 0 to 1
- lat_sign: int32 [8192], replicated, may hold values from 0 to 1
- measurement_site_position: int32 [256], replicated, may hold values from 0 to 8191, as said below
- obs_var: float32 [256], replicated, may hold values from 0.5 to 2
Outputs:
- analysis: float32 [8192, 8192], P('row', 'col')
The draws below stay inside these ranges and needn't reach their ends.
Inputs may be any that keep to these rules, and one draw needn't show every extreme that they name: `measurement_site_position`: distinct cells.
All inputs are finite; a program needn't handle non-finite values.
Results may differ from the reference program's by a relative error of at most 0.00012.
Values sent between devices are 32-bit elements; how exact they have to be, the bound alone decides.
A program may use at most 128 MiB of HBM per device.

```python
import math
import jax
import jax.numpy as jnp
from jax import lax

PARALLEL_STRIPS = 64
MERIDIAN_TOTAL = 128
NOBS = 256
STEPS = 3
STATES = 8192


def draw_covariance(key, part):
    states = PARALLEL_STRIPS * MERIDIAN_TOTAL
    first, second = jax.random.split(jax.random.fold_in(key, 11))
    noise = jax.random.normal(first, (states, states), jnp.float32)
    diagonal = jnp.exp(jax.random.uniform(second, (states,), jnp.float32, 0.0, math.log(4.0)))
    spread = 1.28 / math.sqrt(states) / math.sqrt(2.0)
    return (noise + noise.T) * spread + jnp.diag(diagonal)


def draw_measurement_site_position(key, part):
    states = PARALLEL_STRIPS * MERIDIAN_TOTAL
    order = jax.random.permutation(jax.random.fold_in(key, 5), states)
    return order[:NOBS].astype(jnp.int32)


def with_ends(result, own_key, smallest, high):
    spot = [jax.random.randint(jax.random.fold_in(own_key, axis), (), 0, length) for axis, length in enumerate(result.shape)]
    widest = result.shape.index(max(result.shape))
    next_to = spot[:widest] + [(spot[widest] + 1) % result.shape[widest]] + spot[widest + 1:]
    return result.at[tuple(spot)].set(smallest).at[tuple(next_to)].set(high)


def setup_inputs(seed: int = 0) -> dict:
    key_of = jax.random.split(jax.random.key(seed), 8)
    covariance = draw_covariance(jax.random.fold_in(key_of[7], 71), 0)
    lon_speed = jnp.clip(jax.random.uniform(key_of[1], (STATES,), jnp.float32, 0.05, 0.45), 0.05, 0.45)
    lat_speed = jnp.clip(jax.random.uniform(key_of[2], (STATES,), jnp.float32, 0.05, 0.45), 0.05, 0.45)
    lon_sign = with_ends(jax.random.randint(key_of[3], (STATES,), 0, 2), jax.random.fold_in(key_of[3], 1), 0, 1).astype(jnp.int32)
    lat_sign = with_ends(jax.random.randint(key_of[4], (STATES,), 0, 2), jax.random.fold_in(key_of[4], 1), 0, 1).astype(jnp.int32)
    measurement_site_position = draw_measurement_site_position(jax.random.fold_in(key_of[7], 71), 0)
    obs_var = jnp.clip(jnp.exp(jax.random.uniform(key_of[6], (NOBS,), jnp.float32, math.log(0.5), math.log(2.0))), 0.5, 2.0)
    return {"covariance": covariance, "lon_speed": lon_speed, "lat_speed": lat_speed, "lon_sign": lon_sign, "lat_sign": lat_sign, "measurement_site_position": measurement_site_position, "obs_var": obs_var}


def advect(q, minus, plus, cu, cv, su, sv, lat_axis):
    lon_up = jnp.where(su > 0, jnp.roll(q, 1, lat_axis + 1), jnp.roll(q, -1, lat_axis + 1))
    lat_up = jnp.where(sv > 0, minus, plus)
    return q - cu * (q - lon_up) - cv * (q - lat_up)

def shifted(q, lat_axis):
    count = q.shape[lat_axis]
    zero_shape = list(q.shape)
    zero_shape[lat_axis] = 1
    zeros = jnp.zeros(zero_shape, jnp.float32)
    minus = jnp.concatenate([zeros, lax.slice_in_dim(q, 0, count - 1, axis=lat_axis)], axis=lat_axis)
    plus = jnp.concatenate([lax.slice_in_dim(q, 1, count, axis=lat_axis), zeros], axis=lat_axis)
    return (minus, plus)

def reference(covariance, lon_speed, lat_speed, lon_sign, lat_sign, measurement_site_position, obs_var):
    states = PARALLEL_STRIPS * MERIDIAN_TOTAL
    segment_breadth = min(1024, states)
    row_cu = lon_speed.reshape(PARALLEL_STRIPS, MERIDIAN_TOTAL, 1)
    row_cv = lat_speed.reshape(PARALLEL_STRIPS, MERIDIAN_TOTAL, 1)
    row_su = lon_sign.reshape(PARALLEL_STRIPS, MERIDIAN_TOTAL, 1)
    row_sv = lat_sign.reshape(PARALLEL_STRIPS, MERIDIAN_TOTAL, 1)
    segment_parts = []
    for leading_shift in range(0, states, segment_breadth):
        segment_patch = covariance[:, leading_shift:leading_shift + segment_breadth].reshape(PARALLEL_STRIPS, MERIDIAN_TOTAL, segment_breadth)
        for step in range(STEPS):
            minus, plus = shifted(segment_patch, 0)
            segment_patch = advect(segment_patch, minus, plus, row_cu, row_cv, row_su, row_sv, 0)
        segment_parts.append(segment_patch.reshape(states, segment_breadth))
    predicted_error_matrix = jnp.concatenate(segment_parts, axis=1)
    col_cu = lon_speed.reshape(1, PARALLEL_STRIPS, MERIDIAN_TOTAL)
    col_cv = lat_speed.reshape(1, PARALLEL_STRIPS, MERIDIAN_TOTAL)
    col_su = lon_sign.reshape(1, PARALLEL_STRIPS, MERIDIAN_TOTAL)
    col_sv = lat_sign.reshape(1, PARALLEL_STRIPS, MERIDIAN_TOTAL)
    segment_parts = []
    for leading_shift in range(0, states, segment_breadth):
        segment_patch = predicted_error_matrix[leading_shift:leading_shift + segment_breadth].reshape(segment_breadth, PARALLEL_STRIPS, MERIDIAN_TOTAL)
        for step in range(STEPS):
            minus, plus = shifted(segment_patch, 1)
            segment_patch = advect(segment_patch, minus, plus, col_cu, col_cv, col_su, col_sv, 1)
        segment_parts.append(segment_patch.reshape(segment_breadth, states))
    predicted_error_matrix = jnp.concatenate(segment_parts, axis=0)
    background_product_gain = predicted_error_matrix[:, measurement_site_position]
    measured_background_lines = predicted_error_matrix[measurement_site_position, :]
    hpht = measured_background_lines[:, measurement_site_position]
    innovation = hpht + jnp.diag(obs_var)
    factor = jnp.linalg.cholesky(innovation)
    weights = jax.scipy.linalg.cho_solve((factor, True), measured_background_lines)
    segment_parts = []
    for leading_shift in range(0, states, segment_breadth):
        measurement_correction = jnp.dot(background_product_gain[leading_shift:leading_shift + segment_breadth].astype(jnp.float32), weights.astype(jnp.float32), precision=lax.Precision.HIGHEST, preferred_element_type=jnp.float32)
        segment_parts.append(predicted_error_matrix[leading_shift:leading_shift + segment_breadth] - measurement_correction)
    return jnp.concatenate(segment_parts, axis=0)
```

```python
import functools

import jax
import jax.numpy as jnp
from jax import lax
from jax.experimental import pallas as pl
from jax.experimental.pallas import tpu as pltpu
from jax.sharding import PartitionSpec as P

LON = 128
STEPS = 3
MARGIN = STEPS * LON
VMEM_LIMIT = 48 * 1024 * 1024
HIGHEST = lax.Precision.HIGHEST
HIGH = lax.Precision.HIGH


def params():
    return pltpu.CompilerParams(vmem_limit_bytes=VMEM_LIMIT)


def halos(x, axis, dim):
    count = lax.axis_size(axis)
    size = x.shape[dim]
    before, after = [], []
    left, hop = MARGIN, 1
    while left > 0:
        take = min(left, size)
        tail = lax.slice_in_dim(x, size - take, size, axis=dim)
        head = lax.slice_in_dim(x, 0, take, axis=dim)
        before.insert(0, lax.ppermute(tail, axis, [(i, i + hop) for i in range(count - hop)]))
        after.append(lax.ppermute(head, axis, [(i + hop, i) for i in range(count - hop)]))
        left, hop = left - take, hop + 1
    if len(before) == 1:
        return before[0], after[0]
    return jnp.concatenate(before, axis=dim), jnp.concatenate(after, axis=dim)


def advance(q, minus, plus, cu, cv, su, sv, dim):
    lon = jnp.where(su > 0, pltpu.roll(q, 1, dim), pltpu.roll(q, LON - 1, dim))
    lat = jnp.where(sv > 0, minus, plus)
    return q - cu * (q - lon) - cv * (q - lat)


def row_kernel(bands, x, lo, hi, cu, cv, su, sv, out, buf):
    total = bands + 2 * STEPS

    def raw(k):
        if k < STEPS:
            return lo[k * LON : (k + 1) * LON, :]
        if k < STEPS + bands:
            return x[(k - STEPS) * LON : (k - STEPS + 1) * LON, :]
        k -= STEPS + bands
        return hi[k * LON : (k + 1) * LON, :]

    get = raw
    for s in range(STEPS):
        for k in range(s + 1, total - 1 - s):
            r = slice(k * LON, (k + 1) * LON)
            new = advance(get(k), get(k - 1), get(k + 1), cu[r], cv[r], su[r], sv[r], 0)
            if s == STEPS - 1:
                out[(k - STEPS) * LON : (k - STEPS + 1) * LON, :] = new
            else:
                buf[s, r, :] = new
        get = lambda k, s=s: buf[s, k * LON : (k + 1) * LON, :]


def row_transport(x, lo, hi, coeffs, tiles, column_of):
    rows = x.shape[0]
    wide = rows + 2 * MARGIN
    const = pl.BlockSpec((wide, LON), lambda j: (0, 0))
    return pl.pallas_call(
        functools.partial(row_kernel, rows // LON),
        grid=(tiles,),
        in_specs=[
            pl.BlockSpec((rows, LON), lambda j: (0, column_of(j))),
            pl.BlockSpec((MARGIN, LON), lambda j: (0, j)),
            pl.BlockSpec((MARGIN, LON), lambda j: (0, j)),
            const,
            const,
            const,
            const,
        ],
        out_specs=pl.BlockSpec((rows, LON), lambda j: (0, j)),
        out_shape=jax.ShapeDtypeStruct((rows, tiles * LON), jnp.float32),
        scratch_shapes=[pltpu.VMEM((2, wide, LON), jnp.float32)],
        compiler_params=params(),
        cost_estimate=pl.CostEstimate(
            flops=30 * wide * tiles * LON, bytes_accessed=8 * wide * tiles * LON, transcendentals=0
        ),
    )(x, lo, hi, *coeffs)


def col_steps(raw, total, cu, cv, su, sv, buf, finish):
    get = raw
    for s in range(STEPS):
        for k in range(s + 1, total - 1 - s):
            c = slice(k * LON, (k + 1) * LON)
            new = advance(get(k), get(k - 1), get(k + 1), cu[:, c], cv[:, c], su[:, c], sv[:, c], 1)
            if s == STEPS - 1:
                finish(k - STEPS, new)
            else:
                buf[s, :, c] = new
        get = lambda k, s=s: buf[s, :, k * LON : (k + 1) * LON]


def band_reader(pieces):
    table = [(ref, first + k) for ref, first, n in pieces for k in range(n)]

    def raw(k):
        ref, at = table[k]
        return ref[:, at * LON : (at + 1) * LON]

    return raw, len(table)


def final_kernel(pieces, n, *args):
    refs, (pht, w, cu, cv, su, sv, out, buf) = args[:n], args[n:]
    raw, total = band_reader([(refs[i], f, c) for i, f, c in pieces])
    gain = pht[...]

    def finish(k, new):
        c = slice(k * LON, (k + 1) * LON)
        out[:, c] = new - out[:, c]

    for c in range(0, out.shape[1], 512):
        d = slice(c, min(c + 512, out.shape[1]))
        out[:, d] = jnp.dot(gain, w[:, d], precision=HIGHEST, preferred_element_type=jnp.float32)
    col_steps(raw, total, cu, cv, su, sv, buf, finish)


def weights_kernel(a, lo, hi, inv, cu, cv, su, sv, w, hp, buf):
    bands = a.shape[1] // LON
    raw, total = band_reader([(lo, 0, STEPS), (a, 0, bands), (hi, 0, STEPS)])

    def finish(k, new):
        hp[:, k * LON : (k + 1) * LON] = new

    col_steps(raw, total, cu, cv, su, sv, buf, finish)
    for c in range(0, w.shape[1], 512):
        d = slice(c, min(c + 512, w.shape[1]))
        w[:, d] = jnp.dot(inv[...], hp[:, d], precision=HIGHEST, preferred_element_type=jnp.float32)


def site_kernel(start_ref, site, cu, cv, su, sv, out):
    total = cu.shape[1] // LON
    rows = site.shape[0]
    where = jnp.broadcast_to(site[...] - start_ref[0] + MARGIN, (rows, LON))
    lane = lax.broadcasted_iota(jnp.int32, (rows, LON), 1)
    v = [jnp.where(where == lane + k * LON, 1.0, 0.0) for k in range(total)]
    for s in range(STEPS):
        lo, hi = s + 1, total - 1 - s
        down, up, new = {}, {}, []
        for k in range(lo - 1, hi + 1):
            c = slice(k * LON, (k + 1) * LON)
            t = cv[:, c] * v[k]
            down[k] = jnp.where(sv[:, c] > 0, t, 0.0)
            up[k] = jnp.where(sv[:, c] > 0, 0.0, t)
        for k in range(total):
            if k < lo or k >= hi:
                new.append(v[k])
                continue
            c = slice(k * LON, (k + 1) * LON)
            t = cu[:, c] * v[k]
            west = pltpu.roll(jnp.where(su[:, c] > 0, t, 0.0), LON - 1, 1)
            east = pltpu.roll(jnp.where(su[:, c] > 0, 0.0, t), 1, 1)
            keep = v[k] - t - cv[:, c] * v[k]
            new.append(keep + west + east + down[k + 1] + up[k - 1])
        v = new
    for k in range(STEPS, total - STEPS):
        out[:, (k - STEPS) * LON : (k - STEPS + 1) * LON] = v[k]


def site_rows(site, start, coeffs):
    wide = coeffs[0].shape[1]
    nobs = site.shape[0]
    tile = 8
    const = pl.BlockSpec((1, wide), lambda i, s: (0, 0))
    return pl.pallas_call(
        site_kernel,
        grid_spec=pltpu.PrefetchScalarGridSpec(
            num_scalar_prefetch=1,
            grid=(nobs // tile,),
            in_specs=[pl.BlockSpec((tile, 1), lambda i, s: (i, 0)), const, const, const, const],
            out_specs=pl.BlockSpec((tile, wide - 2 * MARGIN), lambda i, s: (i, 0)),
        ),
        out_shape=jax.ShapeDtypeStruct((nobs, wide - 2 * MARGIN), jnp.float32),
        compiler_params=params(),
    )(start.reshape(1).astype(jnp.int32), site.reshape(nobs, 1), *coeffs)


def sweep_inverse(a):
    n = a.shape[0]
    sub = lax.broadcasted_iota(jnp.int32, (n, n), 0)
    lane = lax.broadcasted_iota(jnp.int32, (n, n), 1)

    def body(_, a):
        for i in range(8):
            r = 1.0 / a[i : i + 1, i : i + 1]
            row = a[i : i + 1, :] * r
            col = a[:, i : i + 1]
            new = jnp.where(lane == i, col * r, a - col * row)
            a = jnp.where(sub == i, jnp.where(lane == i, -r, row), new)
        a = jnp.concatenate([a[8:], a[:8]], axis=0)
        return pltpu.roll(a, n - 8, 1)

    return -lax.fori_loop(0, n // 8, body, a)


def mm(x, y):
    return jnp.dot(x, y, precision=HIGHEST, preferred_element_type=jnp.float32)


def inverse(a):
    n = a.shape[0]
    if n <= LON:
        return sweep_inverse(a)
    h = n // 2
    s12, s22 = a[:h, h:], a[h:, h:]
    i1 = inverse(a[:h, :h])
    x = mm(i1, s12)
    i2 = inverse(s22 - mm(s12.T, x))
    y = mm(x, i2)
    return jnp.concatenate(
        [
            jnp.concatenate([i1 + mm(y, x.T), -y], axis=1),
            jnp.concatenate([-y.T, i2], axis=1),
        ],
        axis=0,
    )


def inverse_kernel(s, r, out):
    n = s.shape[0]
    sub = lax.broadcasted_iota(jnp.int32, (n, n), 0)
    lane = lax.broadcasted_iota(jnp.int32, (n, n), 1)
    a = s[...] + jnp.where(sub == lane, jnp.broadcast_to(r[...], (n, n)), 0.0)
    out[...] = inverse(0.5 * (a + a.T))


def shards(
    covariance, lon_speed, lat_speed, lon_sign, lat_sign, measurement_site_position, obs_var
):
    rows, cols = covariance.shape
    nobs = obs_var.shape[0]
    row_start = lax.axis_index("row") * rows
    col_start = lax.axis_index("col") * cols
    fields = jnp.stack(
        [lon_speed, lat_speed, lon_sign.astype(jnp.float32), lat_sign.astype(jnp.float32)]
    )
    fields = jnp.pad(fields, ((0, 0), (MARGIN, MARGIN)))
    row_fields = lax.dynamic_slice_in_dim(fields, row_start, rows + 2 * MARGIN, axis=1)
    col_fields = lax.dynamic_slice_in_dim(fields, col_start, cols + 2 * MARGIN, axis=1)
    row_lines = [row_fields[i : i + 1] for i in range(4)]
    col_lines = [col_fields[i : i + 1] for i in range(4)]
    row_coeffs = [
        jnp.broadcast_to(row_fields[i][:, None], (rows + 2 * MARGIN, LON)) for i in range(4)
    ]

    tiles = cols // LON
    split = tiles > 2 * STEPS
    if split:
        edge_cols = jnp.concatenate([covariance[:, :MARGIN], covariance[:, cols - MARGIN :]], axis=1) if rows < MARGIN else None
        if edge_cols is None:
            head = jnp.concatenate([covariance[:MARGIN, :MARGIN], covariance[:MARGIN, cols - MARGIN :]], axis=1)
            tail = jnp.concatenate(
                [covariance[rows - MARGIN :, :MARGIN], covariance[rows - MARGIN :, cols - MARGIN :]], axis=1
            )
            count = lax.axis_size("row")
            edge_lo = lax.ppermute(tail, "row", [(i, i + 1) for i in range(count - 1)])
            edge_hi = lax.ppermute(head, "row", [(i + 1, i) for i in range(count - 1)])
        else:
            edge_lo, edge_hi = halos(edge_cols, "row", 0)
        mid_lo, mid_hi = halos(covariance[:, MARGIN : cols - MARGIN], "row", 0)
        skip = tiles - 2 * STEPS
        edges = row_transport(
            covariance, edge_lo, edge_hi, row_coeffs, 2 * STEPS,
            lambda j: jnp.where(j < STEPS, j, j + skip),
        )
        first, last = edges[:, :MARGIN], edges[:, MARGIN:]
        count = lax.axis_size("col")
        left = lax.ppermute(last, "col", [(i, i + 1) for i in range(count - 1)])
        right = lax.ppermute(first, "col", [(i + 1, i) for i in range(count - 1)])
        middle = row_transport(
            covariance, mid_lo, mid_hi, row_coeffs, skip, lambda j: j + STEPS
        )
        arrays = [left, edges, middle, right]
        pieces = [(0, 0, STEPS), (1, 0, STEPS), (2, 0, skip), (1, STEPS, STEPS), (3, 0, STEPS)]
    else:
        lo, hi = halos(covariance, "row", 0)
        whole = row_transport(covariance, lo, hi, row_coeffs, tiles, lambda j: j)
        left, right = halos(whole, "col", 1)
        arrays = [left, whole, right]
        pieces = [(0, 0, STEPS), (1, 0, tiles), (2, 0, STEPS)]

    g_row = site_rows(measurement_site_position, row_start, row_lines)
    g_col = site_rows(measurement_site_position, col_start, col_lines)
    dot = functools.partial(
        lax.dot_general, precision=HIGH, preferred_element_type=jnp.float32
    )
    a_part = dot(g_row, covariance, (((1,), (0,)), ((), ())))
    b_part = dot(covariance, g_col, (((1,), (1,)), ((), ())))
    s_part = lax.dot_general(
        a_part, g_col, (((1,), (1,)), ((), ())), precision=HIGHEST, preferred_element_type=jnp.float32
    )
    s = lax.psum(s_part, ("row", "col"))
    a = lax.psum(a_part, "row")
    b = lax.psum(b_part, "col")
    inv = pl.pallas_call(
        inverse_kernel,
        out_shape=jax.ShapeDtypeStruct((nobs, nobs), jnp.float32),
        compiler_params=params(),
    )(s, obs_var.reshape(1, nobs))
    b_lo, b_hi = halos(b, "row", 0)
    pht = row_transport(b, b_lo, b_hi, row_coeffs, nobs // LON, lambda j: j)
    a_lo, a_hi = halos(a, "col", 1)
    wide = cols + 2 * MARGIN
    w = pl.pallas_call(
        weights_kernel,
        out_shape=jax.ShapeDtypeStruct((nobs, cols), jnp.float32),
        scratch_shapes=[
            pltpu.VMEM((nobs, cols), jnp.float32),
            pltpu.VMEM((2, nobs, wide), jnp.float32),
        ],
        compiler_params=params(),
    )(a, a_lo, a_hi, inv, *col_lines)

    tile = LON
    return pl.pallas_call(
        functools.partial(final_kernel, pieces, len(arrays)),
        grid=(rows // tile,),
        in_specs=[pl.BlockSpec((tile, x.shape[1]), lambda i: (i, 0)) for x in arrays]
        + [
            pl.BlockSpec((tile, nobs), lambda i: (i, 0)),
            pl.BlockSpec((nobs, cols), lambda i: (0, 0)),
        ]
        + [pl.BlockSpec((1, wide), lambda i: (0, 0))] * 4,
        out_specs=pl.BlockSpec((tile, cols), lambda i: (i, 0)),
        out_shape=jax.ShapeDtypeStruct((rows, cols), jnp.float32),
        scratch_shapes=[pltpu.VMEM((2, tile, wide), jnp.float32)],
        compiler_params=params(),
    )(*arrays, pht, w, *col_lines)


def solution(mesh):
    return jax.shard_map(
        shards,
        mesh=mesh,
        in_specs=(P("row", "col"), P(), P(), P(), P(), P(), P()),
        out_specs=P("row", "col"),
        check_vma=False,
    )
```

```python
import functools

import jax
import jax.numpy as jnp
from jax import lax
from jax.experimental import pallas as pl
from jax.experimental.pallas import tpu as pltpu
from jax.sharding import PartitionSpec as P

LON = 128
STEPS = 3
MARGIN = STEPS * LON
VMEM_LIMIT = 48 * 1024 * 1024
HIGHEST = lax.Precision.HIGHEST
HIGH = lax.Precision.HIGH


def params():
    return pltpu.CompilerParams(vmem_limit_bytes=VMEM_LIMIT)


def halos(x, axis, dim):
    count = lax.axis_size(axis)
    size = x.shape[dim]
    before, after = [], []
    left, hop = MARGIN, 1
    while left > 0:
        take = min(left, size)
        tail = lax.slice_in_dim(x, size - take, size, axis=dim)
        head = lax.slice_in_dim(x, 0, take, axis=dim)
        before.insert(0, lax.ppermute(tail, axis, [(i, i + hop) for i in range(count - hop)]))
        after.append(lax.ppermute(head, axis, [(i + hop, i) for i in range(count - hop)]))
        left, hop = left - take, hop + 1
    if len(before) == 1:
        return before[0], after[0]
    return jnp.concatenate(before, axis=dim), jnp.concatenate(after, axis=dim)


def advance(q, minus, plus, cu, cv, su, sv, dim):
    lon = jnp.where(su > 0, pltpu.roll(q, 1, dim), pltpu.roll(q, LON - 1, dim))
    lat = jnp.where(sv > 0, minus, plus)
    return q - cu * (q - lon) - cv * (q - lat)


def row_kernel(bands, x, lo, hi, cu, cv, su, sv, out, buf):
    total = bands + 2 * STEPS

    def raw(k):
        if k < STEPS:
            return lo[k * LON : (k + 1) * LON, :]
        if k < STEPS + bands:
            return x[(k - STEPS) * LON : (k - STEPS + 1) * LON, :]
        k -= STEPS + bands
        return hi[k * LON : (k + 1) * LON, :]

    get = raw
    for s in range(STEPS):
        for k in range(s + 1, total - 1 - s):
            r = slice(k * LON, (k + 1) * LON)
            new = advance(get(k), get(k - 1), get(k + 1), cu[r], cv[r], su[r], sv[r], 0)
            if s == STEPS - 1:
                out[(k - STEPS) * LON : (k - STEPS + 1) * LON, :] = new
            else:
                buf[s, r, :] = new
        get = lambda k, s=s: buf[s, k * LON : (k + 1) * LON, :]


def row_transport(x, lo, hi, coeffs, tiles, column_of):
    rows = x.shape[0]
    wide = rows + 2 * MARGIN
    const = pl.BlockSpec((wide, LON), lambda j: (0, 0))
    return pl.pallas_call(
        functools.partial(row_kernel, rows // LON),
        grid=(tiles,),
        in_specs=[
            pl.BlockSpec((rows, LON), lambda j: (0, column_of(j))),
            pl.BlockSpec((MARGIN, LON), lambda j: (0, j)),
            pl.BlockSpec((MARGIN, LON), lambda j: (0, j)),
            const,
            const,
            const,
            const,
        ],
        out_specs=pl.BlockSpec((rows, LON), lambda j: (0, j)),
        out_shape=jax.ShapeDtypeStruct((rows, tiles * LON), jnp.float32),
        scratch_shapes=[pltpu.VMEM((2, wide, LON), jnp.float32)],
        compiler_params=params(),
        cost_estimate=pl.CostEstimate(
            flops=30 * wide * tiles * LON, bytes_accessed=8 * wide * tiles * LON, transcendentals=0
        ),
    )(x, lo, hi, *coeffs)


def col_steps(raw, total, cu, cv, su, sv, buf, finish):
    get = raw
    for s in range(STEPS):
        for k in range(s + 1, total - 1 - s):
            c = slice(k * LON, (k + 1) * LON)
            new = advance(get(k), get(k - 1), get(k + 1), cu[:, c], cv[:, c], su[:, c], sv[:, c], 1)
            if s == STEPS - 1:
                finish(k - STEPS, new)
            else:
                buf[s, :, c] = new
        get = lambda k, s=s: buf[s, :, k * LON : (k + 1) * LON]


def band_reader(pieces):
    table = [(ref, first + k) for ref, first, n in pieces for k in range(n)]

    def raw(k):
        ref, at = table[k]
        return ref[:, at * LON : (at + 1) * LON]

    return raw, len(table)


def final_kernel(pieces, n, *args):
    refs, (pht, w, cu, cv, su, sv, out, buf) = args[:n], args[n:]
    raw, total = band_reader([(refs[i], f, c) for i, f, c in pieces])
    gain = pht[...]

    def finish(k, new):
        c = slice(k * LON, (k + 1) * LON)
        out[:, c] = new - out[:, c]

    for c in range(0, out.shape[1], 512):
        d = slice(c, min(c + 512, out.shape[1]))
        out[:, d] = jnp.dot(gain, w[:, d], precision=HIGHEST, preferred_element_type=jnp.float32)
    col_steps(raw, total, cu, cv, su, sv, buf, finish)


def weights_kernel(a, lo, hi, inv, cu, cv, su, sv, w, hp, buf):
    bands = a.shape[1] // LON
    raw, total = band_reader([(lo, 0, STEPS), (a, 0, bands), (hi, 0, STEPS)])

    def finish(k, new):
        hp[:, k * LON : (k + 1) * LON] = new

    col_steps(raw, total, cu, cv, su, sv, buf, finish)
    for c in range(0, w.shape[1], 512):
        d = slice(c, min(c + 512, w.shape[1]))
        w[:, d] = jnp.dot(inv[...], hp[:, d], precision=HIGHEST, preferred_element_type=jnp.float32)


def site_kernel(start_ref, site, cu, cv, su, sv, out):
    total = cu.shape[1] // LON
    rows = site.shape[0]
    where = jnp.broadcast_to(site[...] - start_ref[0] + MARGIN, (rows, LON))
    lane = lax.broadcasted_iota(jnp.int32, (rows, LON), 1)
    v = [jnp.where(where == lane + k * LON, 1.0, 0.0) for k in range(total)]
    for s in range(STEPS):
        lo, hi = s + 1, total - 1 - s
        down, up, new = {}, {}, []
        for k in range(lo - 1, hi + 1):
            c = slice(k * LON, (k + 1) * LON)
            t = cv[:, c] * v[k]
            down[k] = jnp.where(sv[:, c] > 0, t, 0.0)
            up[k] = jnp.where(sv[:, c] > 0, 0.0, t)
        for k in range(total):
            if k < lo or k >= hi:
                new.append(v[k])
                continue
            c = slice(k * LON, (k + 1) * LON)
            t = cu[:, c] * v[k]
            west = pltpu.roll(jnp.where(su[:, c] > 0, t, 0.0), LON - 1, 1)
            east = pltpu.roll(jnp.where(su[:, c] > 0, 0.0, t), 1, 1)
            keep = v[k] - t - cv[:, c] * v[k]
            new.append(keep + west + east + down[k + 1] + up[k - 1])
        v = new
    for k in range(STEPS, total - STEPS):
        out[:, (k - STEPS) * LON : (k - STEPS + 1) * LON] = v[k]


def site_rows(site, start, coeffs):
    wide = coeffs[0].shape[1]
    nobs = site.shape[0]
    tile = min(nobs, 64)
    const = pl.BlockSpec((1, wide), lambda i, s: (0, 0))
    return pl.pallas_call(
        site_kernel,
        grid_spec=pltpu.PrefetchScalarGridSpec(
            num_scalar_prefetch=1,
            grid=(nobs // tile,),
            in_specs=[pl.BlockSpec((tile, 1), lambda i, s: (i, 0)), const, const, const, const],
            out_specs=pl.BlockSpec((tile, wide - 2 * MARGIN), lambda i, s: (i, 0)),
        ),
        out_shape=jax.ShapeDtypeStruct((nobs, wide - 2 * MARGIN), jnp.float32),
        compiler_params=params(),
    )(start.reshape(1).astype(jnp.int32), site.reshape(nobs, 1), *coeffs)


def sweep_inverse(a):
    n = a.shape[0]
    sub = lax.broadcasted_iota(jnp.int32, (n, n), 0)
    lane = lax.broadcasted_iota(jnp.int32, (n, n), 1)

    def body(_, a):
        for i in range(8):
            r = 1.0 / a[i : i + 1, i : i + 1]
            row = a[i : i + 1, :] * r
            col = a[:, i : i + 1]
            new = jnp.where(lane == i, col * r, a - col * row)
            a = jnp.where(sub == i, jnp.where(lane == i, -r, row), new)
        a = jnp.concatenate([a[8:], a[:8]], axis=0)
        return pltpu.roll(a, n - 8, 1)

    return -lax.fori_loop(0, n // 8, body, a)


def mm(x, y):
    return jnp.dot(x, y, precision=HIGHEST, preferred_element_type=jnp.float32)


def inverse(a):
    n = a.shape[0]
    if n <= LON:
        return sweep_inverse(a)
    h = n // 2
    s12, s22 = a[:h, h:], a[h:, h:]
    i1 = inverse(a[:h, :h])
    x = mm(i1, s12)
    i2 = inverse(s22 - mm(s12.T, x))
    y = mm(x, i2)
    return jnp.concatenate(
        [
            jnp.concatenate([i1 + mm(y, x.T), -y], axis=1),
            jnp.concatenate([-y.T, i2], axis=1),
        ],
        axis=0,
    )


def inverse_kernel(s, r, out):
    n = s.shape[0]
    sub = lax.broadcasted_iota(jnp.int32, (n, n), 0)
    lane = lax.broadcasted_iota(jnp.int32, (n, n), 1)
    a = s[...] + jnp.where(sub == lane, jnp.broadcast_to(r[...], (n, n)), 0.0)
    out[...] = inverse(0.5 * (a + a.T))


def partner_of(axis, d):
    me = lax.axis_index(axis)
    bit = (me // d) % 2
    return bit, me + d - 2 * d * bit


def exchange(src, dst, axis, peer, sems, i):
    return pltpu.make_async_remote_copy(
        src_ref=src,
        dst_ref=dst,
        send_sem=sems.at[0, i],
        recv_sem=sems.at[1, i],
        device_id={axis: peer},
        device_id_type=pl.DeviceIdType.MESH,
    )


def powers(count):
    return [1 << t for t in range(count.bit_length() - 1)]


def reduce_scatter(acc, rx, axis, count, sems, base):
    rows = acc.shape[0]
    off, size, at = 0, rows, 0
    for t, d in enumerate(powers(count)):
        bit, peer = partner_of(axis, d)
        half = size // 2
        keep = pl.multiple_of(off + bit * half, 8)
        give = pl.multiple_of(off + (1 - bit) * half, 8)
        copy = exchange(
            acc.at[pl.ds(give, half), :], rx.at[at : at + half, :], axis, peer, sems, base + t
        )
        copy.start()
        yield
        copy.wait()
        acc[pl.ds(keep, half), :] += rx[at : at + half, :]
        off, size, at = keep, half, at + half
    return off, size


def all_gather(out, off, size, axis, count, sems, base):
    for t, d in enumerate(reversed(powers(count))):
        bit, peer = partner_of(axis, d)
        part = out.at[pl.ds(pl.multiple_of(off, 8), size), :]
        copy = exchange(part, part, axis, peer, sems, base + t)
        copy.start()
        yield
        copy.wait()
        off, size = off - bit * size, size * 2


def all_reduce(acc, rx, out, axis, count, sems, base):
    off, size = yield from reduce_scatter(acc, rx, axis, count, sems, base)
    own = pl.ds(pl.multiple_of(off, 8), size)
    out[own, :] = acc[own, :]
    yield from all_gather(out, off, size, axis, count, sems, base + len(powers(count)))


def butterfly(acc, rx, sizes, sems, base):
    t = 0
    for axis, count in sizes:
        for d in powers(count):
            _, peer = partner_of(axis, d)
            copy = exchange(acc.at[t], rx.at[t], axis, peer, sems, base + t)
            copy.start()
            yield
            copy.wait()
            acc[t + 1] = acc[t] + rx[t]
            t += 1


def sums_kernel(sizes, a, b, s, a_out, b_out, s_out, a_acc, a_rx, a_all, b_acc, b_rx, b_all, s_acc, s_rx, sems):
    barrier = pltpu.get_barrier_semaphore()
    greeted = 0
    for axis, count in sizes:
        for d in powers(count):
            _, peer = partner_of(axis, d)
            pl.semaphore_signal(
                barrier, inc=1, device_id={axis: peer}, device_id_type=pl.DeviceIdType.MESH
            )
            greeted += 1
    pl.semaphore_wait(barrier, greeted)
    (row, rows), (col, cols) = sizes
    nobs = s.shape[0]
    tiles = a.shape[1] // LON
    s_acc[0] = s[...]
    for k in range(tiles):
        a_acc[k * nobs : (k + 1) * nobs, :] = a[:, k * LON : (k + 1) * LON]
    b_acc[...] = b[...]
    n_row, n_col = len(powers(rows)), len(powers(cols))
    live = [
        butterfly(s_acc, s_rx, sizes, sems, 0),
        all_reduce(a_acc, a_rx, a_all, row, rows, sems, n_row + n_col),
        all_reduce(b_acc, b_rx, b_all, col, cols, sems, 3 * n_row + n_col),
    ]
    while live:
        still = []
        for run in live:
            try:
                next(run)
                still.append(run)
            except StopIteration:
                pass
        live = still
    s_out[...] = s_acc[n_row + n_col]
    b_out[...] = b_all[...]
    for k in range(tiles):
        a_out[:, k * LON : (k + 1) * LON] = a_all[k * nobs : (k + 1) * nobs, :]


def sums(a, b, s):
    sizes = [(axis, lax.axis_size(axis)) for axis in ("row", "col")]
    stages = [len(powers(n)) for _, n in sizes]
    nobs = s.shape[0]
    tall = a.shape[0] * a.shape[1] // LON
    vmem = pl.BlockSpec(memory_space=pltpu.VMEM)
    f32 = jnp.float32
    return pl.pallas_call(
        functools.partial(sums_kernel, sizes),
        in_specs=[vmem] * 3,
        out_specs=[vmem] * 3,
        out_shape=[jax.ShapeDtypeStruct(x.shape, f32) for x in (a, b, s)],
        scratch_shapes=[
            pltpu.VMEM((tall, LON), f32),
            pltpu.VMEM((tall, LON), f32),
            pltpu.VMEM((tall, LON), f32),
            pltpu.VMEM(b.shape, f32),
            pltpu.VMEM(b.shape, f32),
            pltpu.VMEM(b.shape, f32),
            pltpu.VMEM((sum(stages) + 1, nobs, nobs), f32),
            pltpu.VMEM((sum(stages), nobs, nobs), f32),
            pltpu.SemaphoreType.DMA((2, 3 * sum(stages))),
        ],
        compiler_params=pltpu.CompilerParams(
            collective_id=0, has_side_effects=True, vmem_limit_bytes=VMEM_LIMIT
        ),
    )(a, b, s)


def shards(
    covariance, lon_speed, lat_speed, lon_sign, lat_sign, measurement_site_position, obs_var
):
    rows, cols = covariance.shape
    nobs = obs_var.shape[0]
    row_start = lax.axis_index("row") * rows
    col_start = lax.axis_index("col") * cols
    fields = jnp.stack(
        [lon_speed, lat_speed, lon_sign.astype(jnp.float32), lat_sign.astype(jnp.float32)]
    )
    fields = jnp.pad(fields, ((0, 0), (MARGIN, MARGIN)))
    row_fields = lax.dynamic_slice_in_dim(fields, row_start, rows + 2 * MARGIN, axis=1)
    col_fields = lax.dynamic_slice_in_dim(fields, col_start, cols + 2 * MARGIN, axis=1)
    row_lines = [row_fields[i : i + 1] for i in range(4)]
    col_lines = [col_fields[i : i + 1] for i in range(4)]
    row_coeffs = [
        jnp.broadcast_to(row_fields[i][:, None], (rows + 2 * MARGIN, LON)) for i in range(4)
    ]

    tiles = cols // LON
    split = tiles > 2 * STEPS
    if split:
        edge_cols = jnp.concatenate([covariance[:, :MARGIN], covariance[:, cols - MARGIN :]], axis=1) if rows < MARGIN else None
        if edge_cols is None:
            head = jnp.concatenate([covariance[:MARGIN, :MARGIN], covariance[:MARGIN, cols - MARGIN :]], axis=1)
            tail = jnp.concatenate(
                [covariance[rows - MARGIN :, :MARGIN], covariance[rows - MARGIN :, cols - MARGIN :]], axis=1
            )
            count = lax.axis_size("row")
            edge_lo = lax.ppermute(tail, "row", [(i, i + 1) for i in range(count - 1)])
            edge_hi = lax.ppermute(head, "row", [(i + 1, i) for i in range(count - 1)])
        else:
            edge_lo, edge_hi = halos(edge_cols, "row", 0)
        mid_lo, mid_hi = halos(covariance[:, MARGIN : cols - MARGIN], "row", 0)
        skip = tiles - 2 * STEPS
        edges = row_transport(
            covariance, edge_lo, edge_hi, row_coeffs, 2 * STEPS,
            lambda j: jnp.where(j < STEPS, j, j + skip),
        )
        first, last = edges[:, :MARGIN], edges[:, MARGIN:]
        count = lax.axis_size("col")
        left = lax.ppermute(last, "col", [(i, i + 1) for i in range(count - 1)])
        right = lax.ppermute(first, "col", [(i + 1, i) for i in range(count - 1)])
        middle = row_transport(
            covariance, mid_lo, mid_hi, row_coeffs, skip, lambda j: j + STEPS
        )
        arrays = [left, edges, middle, right]
        pieces = [(0, 0, STEPS), (1, 0, STEPS), (2, 0, skip), (1, STEPS, STEPS), (3, 0, STEPS)]
    else:
        lo, hi = halos(covariance, "row", 0)
        whole = row_transport(covariance, lo, hi, row_coeffs, tiles, lambda j: j)
        left, right = halos(whole, "col", 1)
        arrays = [left, whole, right]
        pieces = [(0, 0, STEPS), (1, 0, tiles), (2, 0, STEPS)]

    g_row = site_rows(measurement_site_position, row_start, row_lines)
    g_col = site_rows(measurement_site_position, col_start, col_lines)
    dot = functools.partial(
        lax.dot_general, precision=HIGH, preferred_element_type=jnp.float32
    )
    a_part = dot(g_row, covariance, (((1,), (0,)), ((), ())))
    b_part = dot(covariance, g_col, (((1,), (1,)), ((), ())))
    s_part = lax.dot_general(
        a_part, g_col, (((1,), (1,)), ((), ())), precision=HIGHEST, preferred_element_type=jnp.float32
    )
    a, b, s = sums(a_part, b_part, s_part)
    inv = pl.pallas_call(
        inverse_kernel,
        out_shape=jax.ShapeDtypeStruct((nobs, nobs), jnp.float32),
        compiler_params=params(),
    )(s, obs_var.reshape(1, nobs))
    b_lo, b_hi = halos(b, "row", 0)
    pht = row_transport(b, b_lo, b_hi, row_coeffs, nobs // LON, lambda j: j)
    a_lo, a_hi = halos(a, "col", 1)
    wide = cols + 2 * MARGIN
    w = pl.pallas_call(
        weights_kernel,
        out_shape=jax.ShapeDtypeStruct((nobs, cols), jnp.float32),
        scratch_shapes=[
            pltpu.VMEM((nobs, cols), jnp.float32),
            pltpu.VMEM((2, nobs, wide), jnp.float32),
        ],
        compiler_params=params(),
    )(a, a_lo, a_hi, inv, *col_lines)

    tile = LON
    return pl.pallas_call(
        functools.partial(final_kernel, pieces, len(arrays)),
        grid=(rows // tile,),
        in_specs=[pl.BlockSpec((tile, x.shape[1]), lambda i: (i, 0)) for x in arrays]
        + [
            pl.BlockSpec((tile, nobs), lambda i: (i, 0)),
            pl.BlockSpec((nobs, cols), lambda i: (0, 0)),
        ]
        + [pl.BlockSpec((1, wide), lambda i: (0, 0))] * 4,
        out_specs=pl.BlockSpec((tile, cols), lambda i: (i, 0)),
        out_shape=jax.ShapeDtypeStruct((rows, cols), jnp.float32),
        scratch_shapes=[pltpu.VMEM((2, tile, wide), jnp.float32)],
        compiler_params=params(),
    )(*arrays, pht, w, *col_lines)


def solution(mesh):
    return jax.shard_map(
        shards,
        mesh=mesh,
        in_specs=(P("row", "col"), P(), P(), P(), P(), P(), P()),
        out_specs=P("row", "col"),
        check_vma=False,
    )
```

```python
import functools

import jax
import jax.numpy as jnp
from jax import lax
from jax.experimental import pallas as pl
from jax.experimental.pallas import tpu as pltpu
from jax.sharding import PartitionSpec as P

LON = 128
STEPS = 3
MARGIN = STEPS * LON
VMEM_LIMIT = 48 * 1024 * 1024
HIGHEST = lax.Precision.HIGHEST
HIGH = lax.Precision.HIGH


def params():
    return pltpu.CompilerParams(vmem_limit_bytes=VMEM_LIMIT)


def halos(xs, axis, dim):
    count = lax.axis_size(axis)
    size = xs[0].shape[dim]
    before, after = [], []
    left, hop = MARGIN, 1

    def part(lo, hi):
        return jnp.concatenate([lax.slice_in_dim(x, lo, hi, axis=dim) for x in xs], axis=1 - dim)

    while left > 0:
        take = min(left, size)
        tail, head = part(size - take, size), part(0, take)
        before.insert(0, lax.ppermute(tail, axis, [(i, i + hop) for i in range(count - hop)]))
        after.append(lax.ppermute(head, axis, [(i + hop, i) for i in range(count - hop)]))
        left, hop = left - take, hop + 1
    return jnp.concatenate(before, axis=dim), jnp.concatenate(after, axis=dim)


def advance(q, minus, plus, cu, cv, su, sv, dim):
    if dim == 1:
        lane = lax.broadcasted_iota(jnp.int32, q.shape, 1)
        step = jnp.where(su > 0, LON - 1, 1)
        lon = jnp.take_along_axis(q, (lane + step) & (LON - 1), axis=1, mode="promise_in_bounds")
    else:
        lon = jnp.where(su > 0, pltpu.roll(q, 1, dim), pltpu.roll(q, LON - 1, dim))
    lat = jnp.where(sv > 0, minus, plus)
    return q - cu * (q - lon) - cv * (q - lat)


def row_kernel(bands, x, lo, hi, cu, cv, su, sv, out, buf):
    total = bands + 2 * STEPS

    def raw(k):
        if k < STEPS:
            return lo[k * LON : (k + 1) * LON, :]
        if k < STEPS + bands:
            return x[(k - STEPS) * LON : (k - STEPS + 1) * LON, :]
        k -= STEPS + bands
        return hi[k * LON : (k + 1) * LON, :]

    get = raw
    for s in range(STEPS):
        for k in range(s + 1, total - 1 - s):
            r = slice(k * LON, (k + 1) * LON)
            new = advance(get(k), get(k - 1), get(k + 1), cu[r], cv[r], su[r], sv[r], 0)
            if s == STEPS - 1:
                out[(k - STEPS) * LON : (k - STEPS + 1) * LON, :] = new
            else:
                buf[s, r, :] = new
        get = lambda k, s=s: buf[s, k * LON : (k + 1) * LON, :]


def row_transport(x, lo, hi, coeffs, tiles, column_of):
    rows = x.shape[0]
    wide = rows + 2 * MARGIN
    const = pl.BlockSpec((wide, LON), lambda j: (0, 0))
    return pl.pallas_call(
        functools.partial(row_kernel, rows // LON),
        grid=(tiles,),
        in_specs=[
            pl.BlockSpec((rows, LON), lambda j: (0, column_of(j))),
            pl.BlockSpec((MARGIN, LON), lambda j: (0, j)),
            pl.BlockSpec((MARGIN, LON), lambda j: (0, j)),
            const,
            const,
            const,
            const,
        ],
        out_specs=pl.BlockSpec((rows, LON), lambda j: (0, j)),
        out_shape=jax.ShapeDtypeStruct((rows, tiles * LON), jnp.float32),
        scratch_shapes=[pltpu.VMEM((2, wide, LON), jnp.float32)],
        compiler_params=params(),
        cost_estimate=pl.CostEstimate(
            flops=30 * wide * tiles * LON, bytes_accessed=24 * wide * tiles * LON, transcendentals=0
        ),
    )(x, lo, hi, *coeffs)


def col_steps(raw, total, cu, cv, su, sv, buf, finish):
    get = raw
    for s in range(STEPS):
        for k in range(s + 1, total - 1 - s):
            c = slice(k * LON, (k + 1) * LON)
            new = advance(get(k), get(k - 1), get(k + 1), cu[:, c], cv[:, c], su[:, c], sv[:, c], 1)
            if s == STEPS - 1:
                finish(k - STEPS, new)
            else:
                buf[s, :, c] = new
        get = lambda k, s=s: buf[s, :, k * LON : (k + 1) * LON]


def band_reader(pieces):
    table = [(ref, first + k) for ref, first, n in pieces for k in range(n)]

    def raw(k):
        ref, at = table[k]
        return ref[:, at * LON : (at + 1) * LON]

    return raw, len(table)


def final_kernel(pieces, n, *args):
    refs, (pht, w_hi, w_lo, cu, cv, su, sv, out, buf) = args[:n], args[n:]
    raw, total = band_reader([(refs[i], f, c) for i, f, c in pieces])
    hi, lo = halves(pht[...])
    dot = functools.partial(jnp.dot, preferred_element_type=jnp.float32)

    def finish(k, new):
        c = slice(k * LON, (k + 1) * LON)
        out[:, c] = new - out[:, c]

    for c in range(0, out.shape[1], 512):
        d = slice(c, min(c + 512, out.shape[1]))
        out[:, d] = dot(hi, w_hi[:, d]) + (dot(lo, w_hi[:, d]) + dot(hi, w_lo[:, d]))
    col_steps(raw, total, cu, cv, su, sv, buf, finish)


def weights_kernel(a, inv, cu, cv, su, sv, w_hi, w_lo, hp, buf):
    raw, total = band_reader([(a, 0, a.shape[1] // LON)])

    def finish(k, new):
        hp[:, k * LON : (k + 1) * LON] = new

    col_steps(raw, total, cu, cv, su, sv, buf, finish)
    for c in range(0, hp.shape[1], 512):
        d = slice(c, min(c + 512, hp.shape[1]))
        w_hi[:, d], w_lo[:, d] = halves(mm(inv[...], hp[:, d]))


def site_kernel(start_ref, site, cu, cv, su, sv, out):
    total = cu.shape[1] // LON
    rows = site.shape[0]
    where = jnp.broadcast_to(site[...] - start_ref[0] + MARGIN, (rows, LON))
    lane = lax.broadcasted_iota(jnp.int32, (rows, LON), 1)
    v = [jnp.where(where == lane + k * LON, 1.0, 0.0) for k in range(total)]
    for s in range(STEPS):
        lo, hi = s + 1, total - 1 - s
        down, up, new = {}, {}, []
        for k in range(lo - 1, hi + 1):
            c = slice(k * LON, (k + 1) * LON)
            t = cv[:, c] * v[k]
            down[k] = jnp.where(sv[:, c] > 0, t, 0.0)
            up[k] = jnp.where(sv[:, c] > 0, 0.0, t)
        for k in range(total):
            if k < lo or k >= hi:
                new.append(v[k])
                continue
            c = slice(k * LON, (k + 1) * LON)
            t = cu[:, c] * v[k]
            west = pltpu.roll(jnp.where(su[:, c] > 0, t, 0.0), LON - 1, 1)
            east = pltpu.roll(jnp.where(su[:, c] > 0, 0.0, t), 1, 1)
            keep = v[k] - t - cv[:, c] * v[k]
            new.append(keep + west + east + down[k + 1] + up[k - 1])
        v = new
    for k in range(STEPS, total - STEPS):
        out[:, (k - STEPS) * LON : (k - STEPS + 1) * LON] = v[k]


def site_rows(site, start, coeffs):
    wide = coeffs[0].shape[1]
    nobs = site.shape[0]
    tile = min(nobs, 64)
    const = pl.BlockSpec((1, wide), lambda i, s: (0, 0))
    return pl.pallas_call(
        site_kernel,
        grid_spec=pltpu.PrefetchScalarGridSpec(
            num_scalar_prefetch=1,
            grid=(nobs // tile,),
            in_specs=[pl.BlockSpec((tile, 1), lambda i, s: (i, 0)), const, const, const, const],
            out_specs=pl.BlockSpec((tile, wide - 2 * MARGIN), lambda i, s: (i, 0)),
        ),
        out_shape=jax.ShapeDtypeStruct((nobs, wide - 2 * MARGIN), jnp.float32),
        compiler_params=params(),
    )(start.reshape(1).astype(jnp.int32), site.reshape(nobs, 1), *coeffs)


def sweep_inverse(a, tick):
    n = a.shape[0]
    sub = lax.broadcasted_iota(jnp.int32, (n, n), 0)
    lane = lax.broadcasted_iota(jnp.int32, (n, n), 1)

    def body(_, a):
        for i in range(8):
            r = 1.0 / a[i : i + 1, i : i + 1]
            row = a[i : i + 1, :] * r
            col = a[:, i : i + 1]
            new = jnp.where(lane == i, col * r, a - col * row)
            a = jnp.where(sub == i, jnp.where(lane == i, -r, row), new)
        a = jnp.concatenate([a[8:], a[:8]], axis=0)
        return pltpu.roll(a, n - 8, 1)

    for _ in range(2):
        a = lax.fori_loop(0, n // 16, body, a)
        tick()
    return -a


def halves(x):
    hi = x.astype(jnp.bfloat16)
    return hi, (x - hi.astype(jnp.float32)).astype(jnp.bfloat16)


def mm(x, y):
    return jnp.dot(x, y, precision=HIGHEST, preferred_element_type=jnp.float32)


def inverse(a, tick):
    n = a.shape[0]
    if n <= LON:
        return sweep_inverse(a, tick)
    h = n // 2
    s12, s22 = a[:h, h:], a[h:, h:]
    i1 = inverse(a[:h, :h], tick)
    x = mm(i1, s12)
    i2 = inverse(s22 - mm(s12.T, x), tick)
    y = mm(x, i2)
    return jnp.concatenate(
        [
            jnp.concatenate([i1 + mm(y, x.T), -y], axis=1),
            jnp.concatenate([-y.T, i2], axis=1),
        ],
        axis=0,
    )


def partner_of(axis, d):
    me = lax.axis_index(axis)
    bit = (me // d) % 2
    return bit, me + d - 2 * d * bit


def exchange(src, dst, axis, peer, sems, i):
    return pltpu.make_async_remote_copy(
        src_ref=src,
        dst_ref=dst,
        send_sem=sems.at[0, i],
        recv_sem=sems.at[1, i],
        device_id={axis: peer},
        device_id_type=pl.DeviceIdType.MESH,
    )


def powers(count):
    return [1 << t for t in range(count.bit_length() - 1)]


def reduce_scatter(acc, rx, axis, count, sems, base):
    rows = acc.shape[0]
    off, size, at = 0, rows, 0
    for t, d in enumerate(powers(count)):
        bit, peer = partner_of(axis, d)
        half = size // 2
        keep = pl.multiple_of(off + bit * half, 8)
        give = pl.multiple_of(off + (1 - bit) * half, 8)
        copy = exchange(
            acc.at[pl.ds(give, half), :], rx.at[at : at + half, :], axis, peer, sems, base + t
        )
        copy.start()
        yield
        copy.wait()
        acc[pl.ds(keep, half), :] += rx[at : at + half, :]
        off, size, at = keep, half, at + half
    return off, size


def all_gather(out, off, size, axis, count, sems, base):
    for t, d in enumerate(reversed(powers(count))):
        bit, peer = partner_of(axis, d)
        part = out.at[pl.ds(pl.multiple_of(off, 8), size), :]
        copy = exchange(part, part, axis, peer, sems, base + t)
        copy.start()
        yield
        copy.wait()
        off, size = off - bit * size, size * 2


def all_reduce(acc, rx, out, axis, count, sems, base):
    off, size = yield from reduce_scatter(acc, rx, axis, count, sems, base)
    own = pl.ds(pl.multiple_of(off, 8), size)
    out[own, :] = acc[own, :]
    yield from all_gather(out, off, size, axis, count, sems, base + len(powers(count)))


def small_reduce(acc, rx, part, part_rx, out, first, rest, sems, base):
    off, size, at, i = 0, acc.shape[0], 0, base
    for axis, d in first:
        bit, peer = partner_of(axis, d)
        half = size // 2
        keep = pl.multiple_of(off + bit * half, 8)
        give = pl.multiple_of(off + (1 - bit) * half, 8)
        copy = exchange(
            acc.at[pl.ds(give, half), :], rx.at[at : at + half, :], axis, peer, sems, i
        )
        copy.start()
        yield
        copy.wait()
        acc[pl.ds(keep, half), :] += rx[at : at + half, :]
        off, size, at, i = keep, half, at + half, i + 1
    own = pl.ds(pl.multiple_of(off, 8), size)
    part[0] = acc[own, :]
    for t, (axis, d) in enumerate(rest):
        _, peer = partner_of(axis, d)
        copy = exchange(part.at[t], part_rx.at[t], axis, peer, sems, i)
        copy.start()
        yield
        copy.wait()
        part[t + 1] = part[t] + part_rx[t]
        i += 1
    out[own, :] = part[len(rest)]
    for axis, d in reversed(first):
        bit, peer = partner_of(axis, d)
        ref = out.at[pl.ds(pl.multiple_of(off, 8), size), :]
        copy = exchange(ref, ref, axis, peer, sems, i)
        copy.start()
        yield
        copy.wait()
        off, size, i = off - bit * size, size * 2, i + 1


class Edges:
    def __init__(self, first, last, from_prev, from_next, axis, count, sems, i):
        me = lax.axis_index(axis)
        self.has_next, self.has_prev = me < count - 1, me > 0
        self.into = from_prev, from_next
        self.up = exchange(last, from_prev, axis, jnp.minimum(me + 1, count - 1), sems, i)
        self.down = exchange(first, from_next, axis, jnp.maximum(me - 1, 0), sems, i + 1)

    def start(self):
        @pl.when(self.has_next)
        def _():
            self.up.start()

        @pl.when(self.has_prev)
        def _():
            self.down.start()

    def finish(self):
        @pl.when(self.has_next)
        def _():
            self.up.wait_send()
            self.down.wait_recv()

        @pl.when(self.has_prev)
        def _():
            self.down.wait_send()
            self.up.wait_recv()

        @pl.when(jnp.logical_not(self.has_prev))
        def _():
            self.into[0][...] = jnp.zeros(self.into[0].shape, jnp.float32)

        @pl.when(jnp.logical_not(self.has_next))
        def _():
            self.into[1][...] = jnp.zeros(self.into[1].shape, jnp.float32)


def advance_all(live):
    for run in list(live):
        try:
            next(run)
        except StopIteration:
            live.remove(run)


def sums_kernel(
    sizes, a, b, s, r, edges, a_out, b_out, inv_out, beside,
    a_acc, a_rx, a_all, b_acc, b_rx, b_all, s_acc, s_rx, s_part, s_part_rx, s_all, a_side, sems,
):
    barrier = pltpu.get_barrier_semaphore()
    greeted = 0
    for axis, count in sizes:
        for d in powers(count):
            _, peer = partner_of(axis, d)
            pl.semaphore_signal(
                barrier, inc=1, device_id={axis: peer}, device_id_type=pl.DeviceIdType.MESH
            )
            greeted += 1
    (row, rows), (col, cols) = sizes
    place = lax.axis_index(col)
    for near in ((place + 1) % cols, (place + cols - 1) % cols):
        pl.semaphore_signal(
            barrier, inc=1, device_id={col: near}, device_id_type=pl.DeviceIdType.MESH
        )
        greeted += 1
    pl.semaphore_wait(barrier, greeted)
    nobs = s.shape[0]
    tiles = a.shape[1] // LON
    s_acc[...] = s[...]
    first, rest = small_order(sizes)
    n_row, n_col = len(powers(rows)), len(powers(cols))
    used = 2 * len(first) + len(rest)
    last = used + 2 * (n_row + n_col)
    wide = Edges(
        edges.at[:, :MARGIN], edges.at[:, edges.shape[1] - MARGIN :], beside.at[:, :MARGIN], beside.at[:, MARGIN:],
        col, cols, sems, last,
    )
    small = [small_reduce(s_acc, s_rx, s_part, s_part_rx, s_all, first, rest, sems, 0)]
    advance_all(small)
    wide.start()
    for k in range(tiles):
        a_acc[k * nobs : (k + 1) * nobs, :] = a[:, k * LON : (k + 1) * LON]
    b_acc[...] = b[...]
    large = [
        all_reduce(a_acc, a_rx, a_all, row, rows, sems, used),
        all_reduce(b_acc, b_rx, b_all, col, cols, sems, used + 2 * n_row),
    ]
    advance_all(large)
    step = 0
    while small:
        advance_all(small)
        step += 1
        if step % 3 == 0:
            advance_all(large)
    sub = lax.broadcasted_iota(jnp.int32, (nobs, nobs), 0)
    lane = lax.broadcasted_iota(jnp.int32, (nobs, nobs), 1)
    m = s_all[...] + jnp.where(sub == lane, jnp.broadcast_to(r[...], (nobs, nobs)), 0.0)
    inv_out[...] = inverse(0.5 * (m + m.T), lambda: advance_all(large))
    while large:
        advance_all(large)
    reach = STEPS * nobs
    narrow = Edges(
        a_all.at[:reach, :], a_all.at[(tiles - STEPS) * nobs :, :], a_side.at[0], a_side.at[1],
        col, cols, sems, last + 2,
    )
    narrow.start()
    b_out[...] = b_all[...]
    for k in range(tiles):
        c = MARGIN + k * LON
        a_out[:, c : c + LON] = a_all[k * nobs : (k + 1) * nobs, :]
    narrow.finish()
    for k in range(STEPS):
        c = MARGIN + (tiles + k) * LON
        a_out[:, k * LON : (k + 1) * LON] = a_side[0, k * nobs : (k + 1) * nobs, :]
        a_out[:, c : c + LON] = a_side[1, k * nobs : (k + 1) * nobs, :]
    wide.finish()


def small_order(sizes):
    (row, rows), (col, cols) = sizes
    row_powers = powers(rows)
    first = [(row, d) for d in row_powers[:1]] + [(col, d) for d in powers(cols)]
    return first, [(row, d) for d in row_powers[1:]]


def sums(a, b, s, r, edges):
    sizes = [(axis, lax.axis_size(axis)) for axis in ("row", "col")]
    first, rest = small_order(sizes)
    copies = 2 * len(first) + len(rest) + 2 * sum(len(powers(n)) for _, n in sizes) + 4
    nobs = s.shape[0]
    part = nobs >> len(first)
    tall = a.shape[0] * a.shape[1] // LON
    vmem = pl.BlockSpec(memory_space=pltpu.VMEM)
    f32 = jnp.float32
    return pl.pallas_call(
        functools.partial(sums_kernel, sizes),
        in_specs=[vmem] * 5,
        out_specs=[vmem] * 4,
        out_shape=[
            jax.ShapeDtypeStruct(shape, f32)
            for shape in (
                (nobs, a.shape[1] + 2 * MARGIN), b.shape, s.shape, (b.shape[0], 2 * MARGIN)
            )
        ],
        scratch_shapes=[
            pltpu.VMEM((tall, LON), f32),
            pltpu.VMEM((tall, LON), f32),
            pltpu.VMEM((tall, LON), f32),
            pltpu.VMEM(b.shape, f32),
            pltpu.VMEM(b.shape, f32),
            pltpu.VMEM(b.shape, f32),
            pltpu.VMEM(s.shape, f32),
            pltpu.VMEM(s.shape, f32),
            pltpu.VMEM((len(rest) + 1, part, nobs), f32),
            pltpu.VMEM((max(len(rest), 1), part, nobs), f32),
            pltpu.VMEM(s.shape, f32),
            pltpu.VMEM((2, STEPS * nobs, LON), f32),
            pltpu.SemaphoreType.DMA((2, copies)),
        ],
        compiler_params=pltpu.CompilerParams(
            collective_id=0, has_side_effects=True, vmem_limit_bytes=VMEM_LIMIT
        ),
        cost_estimate=pl.CostEstimate(
            flops=2 * nobs**3, bytes_accessed=80 * a.size * 4, transcendentals=nobs
        ),
    )(a, b, s, r, edges)


def shards(
    covariance, lon_speed, lat_speed, lon_sign, lat_sign, measurement_site_position, obs_var
):
    rows, cols = covariance.shape
    nobs = obs_var.shape[0]
    row_start = lax.axis_index("row") * rows
    col_start = lax.axis_index("col") * cols
    fields = jnp.stack(
        [lon_speed, lat_speed, lon_sign.astype(jnp.float32), lat_sign.astype(jnp.float32)]
    )
    fields = jnp.pad(fields, ((0, 0), (MARGIN, MARGIN)))
    row_fields = lax.dynamic_slice_in_dim(fields, row_start, rows + 2 * MARGIN, axis=1)
    col_fields = lax.dynamic_slice_in_dim(fields, col_start, cols + 2 * MARGIN, axis=1)
    row_lines = [row_fields[i : i + 1] for i in range(4)]
    col_lines = [col_fields[i : i + 1] for i in range(4)]
    row_coeffs = [
        jnp.broadcast_to(row_fields[i][:, None], (rows + 2 * MARGIN, LON)) for i in range(4)
    ]

    tiles = cols // LON
    if tiles > 2 * STEPS:
        ends = slice(0, MARGIN), slice(cols - MARGIN, cols)
        edge_lo, edge_hi = halos([covariance[:, c] for c in ends], "row", 0)
        mid_lo, mid_hi = halos([covariance[:, MARGIN : cols - MARGIN]], "row", 0)
        skip = tiles - 2 * STEPS
        edges = row_transport(
            covariance, edge_lo, edge_hi, row_coeffs, 2 * STEPS,
            lambda j: jnp.where(j < STEPS, j, j + skip),
        )
        middle = row_transport(
            covariance, mid_lo, mid_hi, row_coeffs, skip, lambda j: j + STEPS
        )
        extra = [middle]
        inner = [(1, 0, STEPS), (2, 0, skip), (1, STEPS, STEPS)]
    else:
        edges = row_transport(
            covariance, *halos([covariance], "row", 0), row_coeffs, tiles, lambda j: j
        )
        extra, inner = [], [(1, 0, tiles)]

    g_row = site_rows(measurement_site_position, row_start, row_lines)
    g_col = site_rows(measurement_site_position, col_start, col_lines)
    dot = functools.partial(
        lax.dot_general, precision=HIGH, preferred_element_type=jnp.float32
    )
    a_part = dot(g_row, covariance, (((1,), (0,)), ((), ())))
    b_part = dot(covariance, g_col, (((1,), (1,)), ((), ())))
    s_part = lax.dot_general(
        a_part, g_col, (((1,), (1,)), ((), ())), precision=HIGHEST, preferred_element_type=jnp.float32
    )
    a, b, inv, beside = sums(a_part, b_part, s_part, obs_var.reshape(1, nobs), edges)
    arrays = [beside, edges] + extra
    pieces = [(0, 0, STEPS)] + inner + [(0, STEPS, STEPS)]
    b_lo, b_hi = halos([b], "row", 0)
    pht = row_transport(b, b_lo, b_hi, row_coeffs, nobs // LON, lambda j: j)
    wide = cols + 2 * MARGIN
    w_hi, w_lo = pl.pallas_call(
        weights_kernel,
        out_shape=[jax.ShapeDtypeStruct((nobs, cols), jnp.bfloat16)] * 2,
        scratch_shapes=[
            pltpu.VMEM((nobs, cols), jnp.float32),
            pltpu.VMEM((2, nobs, wide), jnp.float32),
        ],
        compiler_params=params(),
    )(a, inv, *col_lines)

    tile = LON
    return pl.pallas_call(
        functools.partial(final_kernel, pieces, len(arrays)),
        grid=(rows // tile,),
        in_specs=[pl.BlockSpec((tile, x.shape[1]), lambda i: (i, 0)) for x in arrays]
        + [
            pl.BlockSpec((tile, nobs), lambda i: (i, 0)),
            pl.BlockSpec((nobs, cols), lambda i: (0, 0)),
            pl.BlockSpec((nobs, cols), lambda i: (0, 0)),
        ]
        + [pl.BlockSpec((1, wide), lambda i: (0, 0))] * 4,
        out_specs=pl.BlockSpec((tile, cols), lambda i: (i, 0)),
        out_shape=jax.ShapeDtypeStruct((rows, cols), jnp.float32),
        scratch_shapes=[pltpu.VMEM((2, tile, wide), jnp.float32)],
        compiler_params=params(),
    )(*arrays, pht, w_hi, w_lo, *col_lines)


def solution(mesh):
    return jax.shard_map(
        shards,
        mesh=mesh,
        in_specs=(P("row", "col"), P(), P(), P(), P(), P(), P()),
        out_specs=P("row", "col"),
        check_vma=False,
    )
```

```python
import functools

import jax
import jax.numpy as jnp
from jax import lax
from jax.experimental import pallas as pl
from jax.experimental.pallas import tpu as pltpu
from jax.sharding import PartitionSpec as P

LON = 128
STEPS = 3
MARGIN = STEPS * LON
VMEM_LIMIT = 48 * 1024 * 1024
HIGHEST = lax.Precision.HIGHEST
HIGH = lax.Precision.HIGH


def params():
    return pltpu.CompilerParams(vmem_limit_bytes=VMEM_LIMIT)


def halos(xs, axis, dim):
    count = lax.axis_size(axis)
    size = xs[0].shape[dim]
    before, after = [], []
    left, hop = MARGIN, 1

    def part(lo, hi):
        return jnp.concatenate([lax.slice_in_dim(x, lo, hi, axis=dim) for x in xs], axis=1 - dim)

    while left > 0:
        take = min(left, size)
        tail, head = part(size - take, size), part(0, take)
        before.insert(0, lax.ppermute(tail, axis, [(i, i + hop) for i in range(count - hop)]))
        after.append(lax.ppermute(head, axis, [(i + hop, i) for i in range(count - hop)]))
        left, hop = left - take, hop + 1
    return jnp.concatenate(before, axis=dim), jnp.concatenate(after, axis=dim)


def advance(q, minus, plus, cu, cv, su, sv, dim):
    if dim == 1:
        lane = lax.broadcasted_iota(jnp.int32, q.shape, 1)
        step = jnp.where(su > 0, LON - 1, 1)
        lon = jnp.take_along_axis(q, (lane + step) & (LON - 1), axis=1, mode="promise_in_bounds")
    else:
        lon = jnp.where(su > 0, pltpu.roll(q, 1, dim), pltpu.roll(q, LON - 1, dim))
    lat = jnp.where(sv > 0, minus, plus)
    return q - cu * (q - lon) - cv * (q - lat)


def row_kernel(bands, x, lo, hi, cu, cv, su, sv, out, buf):
    total = bands + 2 * STEPS

    def raw(k):
        if k < STEPS:
            return lo[k * LON : (k + 1) * LON, :]
        if k < STEPS + bands:
            return x[(k - STEPS) * LON : (k - STEPS + 1) * LON, :]
        k -= STEPS + bands
        return hi[k * LON : (k + 1) * LON, :]

    get = raw
    for s in range(STEPS):
        for k in range(s + 1, total - 1 - s):
            r = slice(k * LON, (k + 1) * LON)
            new = advance(get(k), get(k - 1), get(k + 1), cu[r], cv[r], su[r], sv[r], 0)
            if s == STEPS - 1:
                out[(k - STEPS) * LON : (k - STEPS + 1) * LON, :] = new
            else:
                buf[s, r, :] = new
        get = lambda k, s=s: buf[s, k * LON : (k + 1) * LON, :]


def row_transport(x, lo, hi, coeffs, tiles, column_of):
    rows = x.shape[0]
    wide = rows + 2 * MARGIN
    const = pl.BlockSpec((wide, LON), lambda j: (0, 0))
    return pl.pallas_call(
        functools.partial(row_kernel, rows // LON),
        grid=(tiles,),
        in_specs=[
            pl.BlockSpec((rows, LON), lambda j: (0, column_of(j))),
            pl.BlockSpec((MARGIN, LON), lambda j: (0, j)),
            pl.BlockSpec((MARGIN, LON), lambda j: (0, j)),
            const,
            const,
            const,
            const,
        ],
        out_specs=pl.BlockSpec((rows, LON), lambda j: (0, j)),
        out_shape=jax.ShapeDtypeStruct((rows, tiles * LON), jnp.float32),
        scratch_shapes=[pltpu.VMEM((2, wide, LON), jnp.float32)],
        compiler_params=params(),
        cost_estimate=pl.CostEstimate(
            flops=30 * wide * tiles * LON, bytes_accessed=24 * wide * tiles * LON, transcendentals=0
        ),
    )(x, lo, hi, *coeffs)


def col_steps(raw, total, cu, cv, su, sv, buf, finish):
    get = raw
    for s in range(STEPS):
        for k in range(s + 1, total - 1 - s):
            c = slice(k * LON, (k + 1) * LON)
            new = advance(get(k), get(k - 1), get(k + 1), cu[:, c], cv[:, c], su[:, c], sv[:, c], 1)
            if s == STEPS - 1:
                finish(k - STEPS, new)
            else:
                buf[s, :, c] = new
        get = lambda k, s=s: buf[s, :, k * LON : (k + 1) * LON]


def band_reader(pieces):
    table = [(ref, first + k) for ref, first, n in pieces for k in range(n)]

    def raw(k):
        ref, at = table[k]
        return ref[:, at * LON : (at + 1) * LON]

    return raw, len(table)


def final_kernel(pieces, n, *args):
    refs, (pht, w_hi, w_lo, cu, cv, su, sv, out, buf) = args[:n], args[n:]
    raw, total = band_reader([(refs[i], f, c) for i, f, c in pieces])
    hi, lo = halves(pht[...])
    dot = functools.partial(jnp.dot, preferred_element_type=jnp.float32)

    def finish(k, new):
        c = slice(k * LON, (k + 1) * LON)
        out[:, c] = new - out[:, c]

    for c in range(0, out.shape[1], 512):
        d = slice(c, min(c + 512, out.shape[1]))
        out[:, d] = dot(hi, w_hi[:, d]) + (dot(lo, w_hi[:, d]) + dot(hi, w_lo[:, d]))
    col_steps(raw, total, cu, cv, su, sv, buf, finish)


def weights_kernel(a, inv, cu, cv, su, sv, w_hi, w_lo, hp, buf):
    raw, total = band_reader([(a, 0, a.shape[1] // LON)])

    def finish(k, new):
        hp[:, k * LON : (k + 1) * LON] = new

    col_steps(raw, total, cu, cv, su, sv, buf, finish)
    for c in range(0, hp.shape[1], 512):
        d = slice(c, min(c + 512, hp.shape[1]))
        w_hi[:, d], w_lo[:, d] = halves(mm(inv[...], hp[:, d]))


def site_kernel(start_ref, site, cu, cv, su, sv, out):
    total = cu.shape[1] // LON
    rows = site.shape[0]
    where = jnp.broadcast_to(site[...] - start_ref[0] + MARGIN, (rows, LON))
    lane = lax.broadcasted_iota(jnp.int32, (rows, LON), 1)
    v = [jnp.where(where == lane + k * LON, 1.0, 0.0) for k in range(total)]
    for s in range(STEPS):
        lo, hi = s + 1, total - 1 - s
        down, up, new = {}, {}, []
        for k in range(lo - 1, hi + 1):
            c = slice(k * LON, (k + 1) * LON)
            t = cv[:, c] * v[k]
            down[k] = jnp.where(sv[:, c] > 0, t, 0.0)
            up[k] = jnp.where(sv[:, c] > 0, 0.0, t)
        for k in range(total):
            if k < lo or k >= hi:
                new.append(v[k])
                continue
            c = slice(k * LON, (k + 1) * LON)
            t = cu[:, c] * v[k]
            west = pltpu.roll(jnp.where(su[:, c] > 0, t, 0.0), LON - 1, 1)
            east = pltpu.roll(jnp.where(su[:, c] > 0, 0.0, t), 1, 1)
            keep = v[k] - t - cv[:, c] * v[k]
            new.append(keep + west + east + down[k + 1] + up[k - 1])
        v = new
    for k in range(STEPS, total - STEPS):
        out[:, (k - STEPS) * LON : (k - STEPS + 1) * LON] = v[k]


def site_rows(site, start, coeffs):
    wide = coeffs[0].shape[1]
    nobs = site.shape[0]
    tile = min(nobs, 64)
    const = pl.BlockSpec((1, wide), lambda i, s: (0, 0))
    return pl.pallas_call(
        site_kernel,
        grid_spec=pltpu.PrefetchScalarGridSpec(
            num_scalar_prefetch=1,
            grid=(nobs // tile,),
            in_specs=[pl.BlockSpec((tile, 1), lambda i, s: (i, 0)), const, const, const, const],
            out_specs=pl.BlockSpec((tile, wide - 2 * MARGIN), lambda i, s: (i, 0)),
        ),
        out_shape=jax.ShapeDtypeStruct((nobs, wide - 2 * MARGIN), jnp.float32),
        compiler_params=params(),
    )(start.reshape(1).astype(jnp.int32), site.reshape(nobs, 1), *coeffs)


def sweep_inverse(a, tick):
    n = a.shape[0]
    sub = lax.broadcasted_iota(jnp.int32, (n, n), 0)
    lane = lax.broadcasted_iota(jnp.int32, (n, n), 1)

    def body(_, a):
        for i in range(8):
            r = 1.0 / a[i : i + 1, i : i + 1]
            row = a[i : i + 1, :] * r
            col = a[:, i : i + 1]
            new = jnp.where(lane == i, col * r, a - col * row)
            a = jnp.where(sub == i, jnp.where(lane == i, -r, row), new)
        a = jnp.concatenate([a[8:], a[:8]], axis=0)
        return pltpu.roll(a, n - 8, 1)

    for _ in range(2):
        a = lax.fori_loop(0, n // 16, body, a)
        tick()
    return -a


def halves(x):
    hi = x.astype(jnp.bfloat16)
    return hi, (x - hi.astype(jnp.float32)).astype(jnp.bfloat16)


def mm(x, y):
    return jnp.dot(x, y, precision=HIGHEST, preferred_element_type=jnp.float32)


def inverse(a, tick):
    n = a.shape[0]
    if n <= LON:
        return sweep_inverse(a, tick)
    h = n // 2
    s12, s22 = a[:h, h:], a[h:, h:]
    i1 = inverse(a[:h, :h], tick)
    x = mm(i1, s12)
    i2 = inverse(s22 - mm(s12.T, x), tick)
    y = mm(x, i2)
    return jnp.concatenate(
        [
            jnp.concatenate([i1 + mm(y, x.T), -y], axis=1),
            jnp.concatenate([-y.T, i2], axis=1),
        ],
        axis=0,
    )


def partner_of(axis, d):
    me = lax.axis_index(axis)
    bit = (me // d) % 2
    return bit, me + d - 2 * d * bit


def exchange(src, dst, axis, peer, sems, i):
    return pltpu.make_async_remote_copy(
        src_ref=src,
        dst_ref=dst,
        send_sem=sems.at[0, i],
        recv_sem=sems.at[1, i],
        device_id={axis: peer},
        device_id_type=pl.DeviceIdType.MESH,
    )


def powers(count):
    return [1 << t for t in range(count.bit_length() - 1)]


def reduce_scatter(acc, rx, axis, count, sems, base):
    rows = acc.shape[0]
    off, size, at = 0, rows, 0
    for t, d in enumerate(powers(count)):
        bit, peer = partner_of(axis, d)
        half = size // 2
        keep = pl.multiple_of(off + bit * half, 8)
        give = pl.multiple_of(off + (1 - bit) * half, 8)
        copy = exchange(
            acc.at[pl.ds(give, half), :], rx.at[at : at + half, :], axis, peer, sems, base + t
        )
        copy.start()
        yield
        copy.wait()
        acc[pl.ds(keep, half), :] += rx[at : at + half, :]
        off, size, at = keep, half, at + half
    return off, size


def all_gather(out, off, size, axis, count, sems, base):
    for t, d in enumerate(reversed(powers(count))):
        bit, peer = partner_of(axis, d)
        part = out.at[pl.ds(pl.multiple_of(off, 8), size), :]
        copy = exchange(part, part, axis, peer, sems, base + t)
        copy.start()
        yield
        copy.wait()
        off, size = off - bit * size, size * 2


def all_reduce(acc, rx, out, axis, count, sems, base):
    off, size = yield from reduce_scatter(acc, rx, axis, count, sems, base)
    own = pl.ds(pl.multiple_of(off, 8), size)
    out[own, :] = acc[own, :]
    yield from all_gather(out, off, size, axis, count, sems, base + len(powers(count)))


def small_reduce(acc, rx, part, part_rx, out, first, rest, sems, base):
    off, size, at, i = 0, acc.shape[0], 0, base
    for axis, d in first:
        bit, peer = partner_of(axis, d)
        half = size // 2
        keep = pl.multiple_of(off + bit * half, 8)
        give = pl.multiple_of(off + (1 - bit) * half, 8)
        copy = exchange(
            acc.at[pl.ds(give, half), :], rx.at[at : at + half, :], axis, peer, sems, i
        )
        copy.start()
        yield
        copy.wait()
        acc[pl.ds(keep, half), :] += rx[at : at + half, :]
        off, size, at, i = keep, half, at + half, i + 1
    own = pl.ds(pl.multiple_of(off, 8), size)
    part[0] = acc[own, :]
    for t, (axis, d) in enumerate(rest):
        _, peer = partner_of(axis, d)
        copy = exchange(part.at[t], part_rx.at[t], axis, peer, sems, i)
        copy.start()
        yield
        copy.wait()
        part[t + 1] = part[t] + part_rx[t]
        i += 1
    out[own, :] = part[len(rest)]
    for axis, d in reversed(first):
        bit, peer = partner_of(axis, d)
        ref = out.at[pl.ds(pl.multiple_of(off, 8), size), :]
        copy = exchange(ref, ref, axis, peer, sems, i)
        copy.start()
        yield
        copy.wait()
        off, size, i = off - bit * size, size * 2, i + 1


class Edges:
    def __init__(self, first, last, from_prev, from_next, axis, count, sems, i):
        me = lax.axis_index(axis)
        self.has_next, self.has_prev = me < count - 1, me > 0
        self.into = from_prev, from_next
        self.up = exchange(last, from_prev, axis, jnp.minimum(me + 1, count - 1), sems, i)
        self.down = exchange(first, from_next, axis, jnp.maximum(me - 1, 0), sems, i + 1)

    def start(self):
        @pl.when(self.has_next)
        def _():
            self.up.start()

        @pl.when(self.has_prev)
        def _():
            self.down.start()

    def finish(self):
        @pl.when(self.has_next)
        def _():
            self.up.wait_send()
            self.down.wait_recv()

        @pl.when(self.has_prev)
        def _():
            self.down.wait_send()
            self.up.wait_recv()

        @pl.when(jnp.logical_not(self.has_prev))
        def _():
            self.into[0][...] = jnp.zeros(self.into[0].shape, jnp.float32)

        @pl.when(jnp.logical_not(self.has_next))
        def _():
            self.into[1][...] = jnp.zeros(self.into[1].shape, jnp.float32)


def advance_all(live):
    for run in list(live):
        try:
            next(run)
        except StopIteration:
            live.remove(run)


def sums_kernel(
    sizes, a, b, s, r, edges, a_out, b_out, inv_out, beside,
    a_acc, a_rx, a_all, b_acc, b_rx, b_all, s_acc, s_rx, s_part, s_part_rx, s_all, a_side, sems,
):
    barrier = pltpu.get_barrier_semaphore()
    greeted = 0
    for axis, count in sizes:
        for d in powers(count):
            _, peer = partner_of(axis, d)
            pl.semaphore_signal(
                barrier, inc=1, device_id={axis: peer}, device_id_type=pl.DeviceIdType.MESH
            )
            greeted += 1
    (row, rows), (col, cols) = sizes
    place = lax.axis_index(col)
    for near in ((place + 1) % cols, (place + cols - 1) % cols):
        pl.semaphore_signal(
            barrier, inc=1, device_id={col: near}, device_id_type=pl.DeviceIdType.MESH
        )
        greeted += 1
    pl.semaphore_wait(barrier, greeted)
    nobs = s.shape[0]
    tiles = a.shape[1] // LON
    s_acc[...] = s[...]
    first, rest = small_order(sizes)
    n_row, n_col = len(powers(rows)), len(powers(cols))
    used = 2 * len(first) + len(rest)
    last = used + 2 * (n_row + n_col)
    wide = Edges(
        edges.at[:, :MARGIN], edges.at[:, edges.shape[1] - MARGIN :], beside.at[:, :MARGIN], beside.at[:, MARGIN:],
        col, cols, sems, last,
    )
    small = [small_reduce(s_acc, s_rx, s_part, s_part_rx, s_all, first, rest, sems, 0)]
    advance_all(small)
    for k in range(tiles):
        a_acc[k * nobs : (k + 1) * nobs, :] = a[:, k * LON : (k + 1) * LON]
    b_acc[...] = b[...]
    large = [all_reduce(a_acc, a_rx, a_all, row, rows, sems, used)]
    other = [all_reduce(b_acc, b_rx, b_all, col, cols, sems, used + 2 * n_row)]
    advance_all(large)
    advance_all(other)
    step = 0
    while small:
        advance_all(small)
        step += 1
        if step % 2 == 0:
            advance_all(other)
        if step % 3 == 0:
            advance_all(large)
    while other:
        advance_all(other)
    wide.start()
    sub = lax.broadcasted_iota(jnp.int32, (nobs, nobs), 0)
    lane = lax.broadcasted_iota(jnp.int32, (nobs, nobs), 1)
    m = s_all[...] + jnp.where(sub == lane, jnp.broadcast_to(r[...], (nobs, nobs)), 0.0)
    inv_out[...] = inverse(0.5 * (m + m.T), lambda: advance_all(large))
    while large:
        advance_all(large)
    reach = STEPS * nobs
    narrow = Edges(
        a_all.at[:reach, :], a_all.at[(tiles - STEPS) * nobs :, :], a_side.at[0], a_side.at[1],
        col, cols, sems, last + 2,
    )
    narrow.start()
    b_out[...] = b_all[...]
    for k in range(tiles):
        c = MARGIN + k * LON
        a_out[:, c : c + LON] = a_all[k * nobs : (k + 1) * nobs, :]
    narrow.finish()
    for k in range(STEPS):
        c = MARGIN + (tiles + k) * LON
        a_out[:, k * LON : (k + 1) * LON] = a_side[0, k * nobs : (k + 1) * nobs, :]
        a_out[:, c : c + LON] = a_side[1, k * nobs : (k + 1) * nobs, :]
    wide.finish()


def small_order(sizes):
    (row, rows), (col, cols) = sizes
    row_powers = powers(rows)
    first = [(row, d) for d in row_powers[:1]] + [(col, d) for d in powers(cols)]
    return first, [(row, d) for d in row_powers[1:]]


def sums(a, b, s, r, edges):
    sizes = [(axis, lax.axis_size(axis)) for axis in ("row", "col")]
    first, rest = small_order(sizes)
    copies = 2 * len(first) + len(rest) + 2 * sum(len(powers(n)) for _, n in sizes) + 4
    nobs = s.shape[0]
    part = nobs >> len(first)
    tall = a.shape[0] * a.shape[1] // LON
    vmem = pl.BlockSpec(memory_space=pltpu.VMEM)
    f32 = jnp.float32
    return pl.pallas_call(
        functools.partial(sums_kernel, sizes),
        in_specs=[vmem] * 5,
        out_specs=[vmem] * 4,
        out_shape=[
            jax.ShapeDtypeStruct(shape, f32)
            for shape in (
                (nobs, a.shape[1] + 2 * MARGIN), b.shape, s.shape, (b.shape[0], 2 * MARGIN)
            )
        ],
        scratch_shapes=[
            pltpu.VMEM((tall, LON), f32),
            pltpu.VMEM((tall, LON), f32),
            pltpu.VMEM((tall, LON), f32),
            pltpu.VMEM(b.shape, f32),
            pltpu.VMEM(b.shape, f32),
            pltpu.VMEM(b.shape, f32),
            pltpu.VMEM(s.shape, f32),
            pltpu.VMEM(s.shape, f32),
            pltpu.VMEM((len(rest) + 1, part, nobs), f32),
            pltpu.VMEM((max(len(rest), 1), part, nobs), f32),
            pltpu.VMEM(s.shape, f32),
            pltpu.VMEM((2, STEPS * nobs, LON), f32),
            pltpu.SemaphoreType.DMA((2, copies)),
        ],
        compiler_params=pltpu.CompilerParams(
            collective_id=0, has_side_effects=True, vmem_limit_bytes=VMEM_LIMIT
        ),
        cost_estimate=pl.CostEstimate(
            flops=2 * nobs**3, bytes_accessed=80 * a.size * 4, transcendentals=nobs
        ),
    )(a, b, s, r, edges)


def shards(
    covariance, lon_speed, lat_speed, lon_sign, lat_sign, measurement_site_position, obs_var
):
    rows, cols = covariance.shape
    nobs = obs_var.shape[0]
    row_start = lax.axis_index("row") * rows
    col_start = lax.axis_index("col") * cols
    fields = jnp.stack(
        [lon_speed, lat_speed, lon_sign.astype(jnp.float32), lat_sign.astype(jnp.float32)]
    )
    fields = jnp.pad(fields, ((0, 0), (MARGIN, MARGIN)))
    row_fields = lax.dynamic_slice_in_dim(fields, row_start, rows + 2 * MARGIN, axis=1)
    col_fields = lax.dynamic_slice_in_dim(fields, col_start, cols + 2 * MARGIN, axis=1)
    row_lines = [row_fields[i : i + 1] for i in range(4)]
    col_lines = [col_fields[i : i + 1] for i in range(4)]
    row_coeffs = [
        jnp.broadcast_to(row_fields[i][:, None], (rows + 2 * MARGIN, LON)) for i in range(4)
    ]

    tiles = cols // LON
    if tiles > 2 * STEPS:
        ends = slice(0, MARGIN), slice(cols - MARGIN, cols)
        edge_lo, edge_hi = halos([covariance[:, c] for c in ends], "row", 0)
        mid_lo, mid_hi = halos([covariance[:, MARGIN : cols - MARGIN]], "row", 0)
        skip = tiles - 2 * STEPS
        edges = row_transport(
            covariance, edge_lo, edge_hi, row_coeffs, 2 * STEPS,
            lambda j: jnp.where(j < STEPS, j, j + skip),
        )
        middle = row_transport(
            covariance, mid_lo, mid_hi, row_coeffs, skip, lambda j: j + STEPS
        )
        extra = [middle]
        inner = [(1, 0, STEPS), (2, 0, skip), (1, STEPS, STEPS)]
    else:
        edges = row_transport(
            covariance, *halos([covariance], "row", 0), row_coeffs, tiles, lambda j: j
        )
        extra, inner = [], [(1, 0, tiles)]

    g_row = site_rows(measurement_site_position, row_start, row_lines)
    g_col = site_rows(measurement_site_position, col_start, col_lines)
    dot = functools.partial(
        lax.dot_general, precision=HIGH, preferred_element_type=jnp.float32
    )
    a_part = dot(g_row, covariance, (((1,), (0,)), ((), ())))
    b_part = dot(covariance, g_col, (((1,), (1,)), ((), ())))
    s_part = lax.dot_general(
        a_part, g_col, (((1,), (1,)), ((), ())), precision=HIGHEST, preferred_element_type=jnp.float32
    )
    a, b, inv, beside = sums(a_part, b_part, s_part, obs_var.reshape(1, nobs), edges)
    arrays = [beside, edges] + extra
    pieces = [(0, 0, STEPS)] + inner + [(0, STEPS, STEPS)]
    b_lo, b_hi = halos([b], "row", 0)
    pht = row_transport(b, b_lo, b_hi, row_coeffs, nobs // LON, lambda j: j)
    wide = cols + 2 * MARGIN
    w_hi, w_lo = pl.pallas_call(
        weights_kernel,
        out_shape=[jax.ShapeDtypeStruct((nobs, cols), jnp.bfloat16)] * 2,
        scratch_shapes=[
            pltpu.VMEM((nobs, cols), jnp.float32),
            pltpu.VMEM((2, nobs, wide), jnp.float32),
        ],
        compiler_params=params(),
    )(a, inv, *col_lines)

    tile = LON
    return pl.pallas_call(
        functools.partial(final_kernel, pieces, len(arrays)),
        grid=(rows // tile,),
        in_specs=[pl.BlockSpec((tile, x.shape[1]), lambda i: (i, 0)) for x in arrays]
        + [
            pl.BlockSpec((tile, nobs), lambda i: (i, 0)),
            pl.BlockSpec((nobs, cols), lambda i: (0, 0)),
            pl.BlockSpec((nobs, cols), lambda i: (0, 0)),
        ]
        + [pl.BlockSpec((1, wide), lambda i: (0, 0))] * 4,
        out_specs=pl.BlockSpec((tile, cols), lambda i: (i, 0)),
        out_shape=jax.ShapeDtypeStruct((rows, cols), jnp.float32),
        scratch_shapes=[pltpu.VMEM((2, tile, wide), jnp.float32)],
        compiler_params=params(),
    )(*arrays, pht, w_hi, w_lo, *col_lines)


def solution(mesh):
    return jax.shard_map(
        shards,
        mesh=mesh,
        in_specs=(P("row", "col"), P(), P(), P(), P(), P(), P()),
        out_specs=P("row", "col"),
        check_vma=False,
    )
```

```python
import functools

import jax
import jax.numpy as jnp
from jax import lax
from jax.experimental import pallas as pl
from jax.experimental.pallas import tpu as pltpu
from jax.sharding import PartitionSpec as P

LON = 128
STEPS = 3
MARGIN = STEPS * LON
VMEM_LIMIT = 48 * 1024 * 1024
HIGHEST = lax.Precision.HIGHEST
HIGH = lax.Precision.HIGH


def params():
    return pltpu.CompilerParams(vmem_limit_bytes=VMEM_LIMIT)


def halos(xs, axis, dim):
    count = lax.axis_size(axis)
    size = xs[0].shape[dim]
    before, after = [], []
    left, hop = MARGIN, 1

    def part(lo, hi):
        return jnp.concatenate([lax.slice_in_dim(x, lo, hi, axis=dim) for x in xs], axis=1 - dim)

    while left > 0:
        take = min(left, size)
        tail, head = part(size - take, size), part(0, take)
        before.insert(0, lax.ppermute(tail, axis, [(i, i + hop) for i in range(count - hop)]))
        after.append(lax.ppermute(head, axis, [(i + hop, i) for i in range(count - hop)]))
        left, hop = left - take, hop + 1
    return jnp.concatenate(before, axis=dim), jnp.concatenate(after, axis=dim)


def advance(q, minus, plus, cu, cv, su, sv, dim):
    if dim == 1:
        lane = lax.broadcasted_iota(jnp.int32, q.shape, 1)
        step = jnp.where(su > 0, LON - 1, 1)
        lon = jnp.take_along_axis(q, (lane + step) & (LON - 1), axis=1, mode="promise_in_bounds")
    else:
        lon = jnp.where(su > 0, pltpu.roll(q, 1, dim), pltpu.roll(q, LON - 1, dim))
    lat = jnp.where(sv > 0, minus, plus)
    return q - cu * (q - lon) - cv * (q - lat)


def row_kernel(bands, x, lo, hi, cu, cv, su, sv, out, buf):
    total = bands + 2 * STEPS

    def raw(k):
        if k < STEPS:
            return lo[k * LON : (k + 1) * LON, :]
        if k < STEPS + bands:
            return x[(k - STEPS) * LON : (k - STEPS + 1) * LON, :]
        k -= STEPS + bands
        return hi[k * LON : (k + 1) * LON, :]

    get = raw
    for s in range(STEPS):
        for k in range(s + 1, total - 1 - s):
            r = slice(k * LON, (k + 1) * LON)
            new = advance(get(k), get(k - 1), get(k + 1), cu[r], cv[r], su[r], sv[r], 0)
            if s == STEPS - 1:
                out[(k - STEPS) * LON : (k - STEPS + 1) * LON, :] = new
            else:
                buf[s, r, :] = new
        get = lambda k, s=s: buf[s, k * LON : (k + 1) * LON, :]


def row_transport(x, lo, hi, coeffs, tiles, column_of):
    rows = x.shape[0]
    wide = rows + 2 * MARGIN
    const = pl.BlockSpec((wide, LON), lambda j: (0, 0))
    return pl.pallas_call(
        functools.partial(row_kernel, rows // LON),
        grid=(tiles,),
        in_specs=[
            pl.BlockSpec((rows, LON), lambda j: (0, column_of(j))),
            pl.BlockSpec((MARGIN, LON), lambda j: (0, j)),
            pl.BlockSpec((MARGIN, LON), lambda j: (0, j)),
            const,
            const,
            const,
            const,
        ],
        out_specs=pl.BlockSpec((rows, LON), lambda j: (0, j)),
        out_shape=jax.ShapeDtypeStruct((rows, tiles * LON), jnp.float32),
        scratch_shapes=[pltpu.VMEM((2, wide, LON), jnp.float32)],
        compiler_params=params(),
        cost_estimate=pl.CostEstimate(
            flops=30 * wide * tiles * LON, bytes_accessed=24 * wide * tiles * LON, transcendentals=0
        ),
    )(x, lo, hi, *coeffs)


def col_steps(raw, total, cu, cv, su, sv, buf, finish):
    get = raw
    for s in range(STEPS):
        for k in range(s + 1, total - 1 - s):
            c = slice(k * LON, (k + 1) * LON)
            new = advance(get(k), get(k - 1), get(k + 1), cu[:, c], cv[:, c], su[:, c], sv[:, c], 1)
            if s == STEPS - 1:
                finish(k - STEPS, new)
            else:
                buf[s, :, c] = new
        get = lambda k, s=s: buf[s, :, k * LON : (k + 1) * LON]


def band_reader(pieces):
    table = [(ref, first + k) for ref, first, n in pieces for k in range(n)]

    def raw(k):
        ref, at = table[k]
        return ref[:, at * LON : (at + 1) * LON]

    return raw, len(table)


def final_kernel(pieces, n, *args):
    refs, (pht, w_hi, w_lo, cu, cv, su, sv, out, buf) = args[:n], args[n:]
    raw, total = band_reader([(refs[i], f, c) for i, f, c in pieces])
    hi, lo = halves(pht[...])
    dot = functools.partial(jnp.dot, preferred_element_type=jnp.float32)

    def finish(k, new):
        c = slice(k * LON, (k + 1) * LON)
        out[:, c] = new - out[:, c]

    for c in range(0, out.shape[1], 512):
        d = slice(c, min(c + 512, out.shape[1]))
        out[:, d] = dot(hi, w_hi[:, d]) + (dot(lo, w_hi[:, d]) + dot(hi, w_lo[:, d]))
    col_steps(raw, total, cu, cv, su, sv, buf, finish)


def weights_kernel(a, inv, cu, cv, su, sv, w_hi, w_lo, hp, buf):
    raw, total = band_reader([(a, 0, a.shape[1] // LON)])

    def finish(k, new):
        hp[:, k * LON : (k + 1) * LON] = new

    col_steps(raw, total, cu, cv, su, sv, buf, finish)
    for c in range(0, hp.shape[1], 512):
        d = slice(c, min(c + 512, hp.shape[1]))
        w_hi[:, d], w_lo[:, d] = halves(mm(inv[...], hp[:, d]))


def site_kernel(start_ref, site, cu, cv, su, sv, out):
    total = cu.shape[1] // LON
    rows = site.shape[0]
    where = jnp.broadcast_to(site[...] - start_ref[0] + MARGIN, (rows, LON))
    lane = lax.broadcasted_iota(jnp.int32, (rows, LON), 1)
    v = [jnp.where(where == lane + k * LON, 1.0, 0.0) for k in range(total)]
    for s in range(STEPS):
        lo, hi = s + 1, total - 1 - s
        down, up, new = {}, {}, []
        for k in range(lo - 1, hi + 1):
            c = slice(k * LON, (k + 1) * LON)
            t = cv[:, c] * v[k]
            down[k] = jnp.where(sv[:, c] > 0, t, 0.0)
            up[k] = jnp.where(sv[:, c] > 0, 0.0, t)
        for k in range(total):
            if k < lo or k >= hi:
                new.append(v[k])
                continue
            c = slice(k * LON, (k + 1) * LON)
            t = cu[:, c] * v[k]
            west = pltpu.roll(jnp.where(su[:, c] > 0, t, 0.0), LON - 1, 1)
            east = pltpu.roll(jnp.where(su[:, c] > 0, 0.0, t), 1, 1)
            keep = v[k] - t - cv[:, c] * v[k]
            new.append(keep + west + east + down[k + 1] + up[k - 1])
        v = new
    for k in range(STEPS, total - STEPS):
        out[:, (k - STEPS) * LON : (k - STEPS + 1) * LON] = v[k]


def site_rows(site, start, coeffs):
    wide = coeffs[0].shape[1]
    nobs = site.shape[0]
    tile = min(nobs, 64)
    const = pl.BlockSpec((1, wide), lambda i, s: (0, 0))
    return pl.pallas_call(
        site_kernel,
        grid_spec=pltpu.PrefetchScalarGridSpec(
            num_scalar_prefetch=1,
            grid=(nobs // tile,),
            in_specs=[pl.BlockSpec((tile, 1), lambda i, s: (i, 0)), const, const, const, const],
            out_specs=pl.BlockSpec((tile, wide - 2 * MARGIN), lambda i, s: (i, 0)),
        ),
        out_shape=jax.ShapeDtypeStruct((nobs, wide - 2 * MARGIN), jnp.float32),
        compiler_params=params(),
    )(start.reshape(1).astype(jnp.int32), site.reshape(nobs, 1), *coeffs)


def sweep_inverse(a, tick):
    n = a.shape[0]
    sub = lax.broadcasted_iota(jnp.int32, (n, n), 0)
    lane = lax.broadcasted_iota(jnp.int32, (n, n), 1)

    def body(_, a):
        for i in range(8):
            r = 1.0 / a[i : i + 1, i : i + 1]
            row = a[i : i + 1, :] * r
            col = a[:, i : i + 1]
            new = jnp.where(lane == i, col * r, a - col * row)
            a = jnp.where(sub == i, jnp.where(lane == i, -r, row), new)
        a = jnp.concatenate([a[8:], a[:8]], axis=0)
        return pltpu.roll(a, n - 8, 1)

    for _ in range(2):
        a = lax.fori_loop(0, n // 16, body, a)
        tick()
    return -a


def halves(x):
    hi = x.astype(jnp.bfloat16)
    return hi, (x - hi.astype(jnp.float32)).astype(jnp.bfloat16)


def mm(x, y):
    return jnp.dot(x, y, precision=HIGHEST, preferred_element_type=jnp.float32)


def inverse(a, tick):
    n = a.shape[0]
    if n <= LON:
        return sweep_inverse(a, tick)
    h = n // 2
    s12, s22 = a[:h, h:], a[h:, h:]
    i1 = inverse(a[:h, :h], tick)
    x = mm(i1, s12)
    i2 = inverse(s22 - mm(s12.T, x), tick)
    y = mm(x, i2)
    return jnp.concatenate(
        [
            jnp.concatenate([i1 + mm(y, x.T), -y], axis=1),
            jnp.concatenate([-y.T, i2], axis=1),
        ],
        axis=0,
    )


def partner_of(axis, d):
    me = lax.axis_index(axis)
    bit = (me // d) % 2
    return bit, me + d - 2 * d * bit


def exchange(src, dst, axis, peer, sems, i):
    return pltpu.make_async_remote_copy(
        src_ref=src,
        dst_ref=dst,
        send_sem=sems.at[0, i],
        recv_sem=sems.at[1, i],
        device_id={axis: peer},
        device_id_type=pl.DeviceIdType.MESH,
    )


def powers(count):
    return [1 << t for t in range(count.bit_length() - 1)]


def reduce_scatter(acc, rx, axis, count, sems, base):
    rows = acc.shape[0]
    off, size, at = 0, rows, 0
    for t, d in enumerate(powers(count)):
        bit, peer = partner_of(axis, d)
        half = size // 2
        keep = pl.multiple_of(off + bit * half, 8)
        give = pl.multiple_of(off + (1 - bit) * half, 8)
        copy = exchange(
            acc.at[pl.ds(give, half), :], rx.at[at : at + half, :], axis, peer, sems, base + t
        )
        copy.start()
        yield
        copy.wait()
        acc[pl.ds(keep, half), :] += rx[at : at + half, :]
        off, size, at = keep, half, at + half
    return off, size


def all_gather(out, off, size, axis, count, sems, base):
    for t, d in enumerate(reversed(powers(count))):
        bit, peer = partner_of(axis, d)
        part = out.at[pl.ds(pl.multiple_of(off, 8), size), :]
        copy = exchange(part, part, axis, peer, sems, base + t)
        copy.start()
        yield
        copy.wait()
        off, size = off - bit * size, size * 2


def all_reduce(acc, rx, out, axis, count, sems, base):
    off, size = yield from reduce_scatter(acc, rx, axis, count, sems, base)
    own = pl.ds(pl.multiple_of(off, 8), size)
    out[own, :] = acc[own, :]
    yield from all_gather(out, off, size, axis, count, sems, base + len(powers(count)))


def small_reduce(acc, rx, part, part_rx, out, first, rest, sems, base):
    off, size, at, i = 0, acc.shape[0], 0, base
    for axis, d in first:
        bit, peer = partner_of(axis, d)
        half = size // 2
        keep = pl.multiple_of(off + bit * half, 8)
        give = pl.multiple_of(off + (1 - bit) * half, 8)
        copy = exchange(
            acc.at[pl.ds(give, half), :], rx.at[at : at + half, :], axis, peer, sems, i
        )
        copy.start()
        yield
        copy.wait()
        acc[pl.ds(keep, half), :] += rx[at : at + half, :]
        off, size, at, i = keep, half, at + half, i + 1
    own = pl.ds(pl.multiple_of(off, 8), size)
    part[0] = acc[own, :]
    for t, (axis, d) in enumerate(rest):
        _, peer = partner_of(axis, d)
        copy = exchange(part.at[t], part_rx.at[t], axis, peer, sems, i)
        copy.start()
        yield
        copy.wait()
        part[t + 1] = part[t] + part_rx[t]
        i += 1
    out[own, :] = part[len(rest)]
    for axis, d in reversed(first):
        bit, peer = partner_of(axis, d)
        ref = out.at[pl.ds(pl.multiple_of(off, 8), size), :]
        copy = exchange(ref, ref, axis, peer, sems, i)
        copy.start()
        yield
        copy.wait()
        off, size, i = off - bit * size, size * 2, i + 1


class Edges:
    def __init__(self, first, last, from_prev, from_next, axis, count, sems, i):
        me = lax.axis_index(axis)
        self.has_next, self.has_prev = me < count - 1, me > 0
        self.into = from_prev, from_next
        self.up = exchange(last, from_prev, axis, jnp.minimum(me + 1, count - 1), sems, i)
        self.down = exchange(first, from_next, axis, jnp.maximum(me - 1, 0), sems, i + 1)

    def start(self):
        @pl.when(self.has_next)
        def _():
            self.up.start()

        @pl.when(self.has_prev)
        def _():
            self.down.start()

    def finish(self):
        @pl.when(self.has_next)
        def _():
            self.up.wait_send()
            self.down.wait_recv()

        @pl.when(self.has_prev)
        def _():
            self.down.wait_send()
            self.up.wait_recv()

        @pl.when(jnp.logical_not(self.has_prev))
        def _():
            self.into[0][...] = jnp.zeros(self.into[0].shape, jnp.float32)

        @pl.when(jnp.logical_not(self.has_next))
        def _():
            self.into[1][...] = jnp.zeros(self.into[1].shape, jnp.float32)


def advance_all(live):
    for run in list(live):
        try:
            next(run)
        except StopIteration:
            live.remove(run)


def sums_kernel(
    sizes, fits, a, b, s, r, beside, a_out, b_out, inv_out, *rest_refs,
):
    corners, scratch = rest_refs[: 2 * fits], rest_refs[2 * fits :]
    (
        a_acc, a_rx, a_all, b_acc, b_rx, b_all, s_acc, s_rx, s_part, s_part_rx, s_all, a_side, sems,
    ) = scratch
    barrier = pltpu.get_barrier_semaphore()
    greeted = 0
    for axis, count in sizes:
        for d in powers(count):
            _, peer = partner_of(axis, d)
            pl.semaphore_signal(
                barrier, inc=1, device_id={axis: peer}, device_id_type=pl.DeviceIdType.MESH
            )
            greeted += 1
    (row, rows), (col, cols) = sizes
    for axis, count in sizes:
        place = lax.axis_index(axis)
        for near in ((place + 1) % count, (place + count - 1) % count):
            pl.semaphore_signal(
                barrier, inc=1, device_id={axis: near}, device_id_type=pl.DeviceIdType.MESH
            )
            greeted += 1
    pl.semaphore_wait(barrier, greeted)
    nobs = s.shape[0]
    tiles = a.shape[1] // LON
    s_acc[...] = s[...]
    first, rest = small_order(sizes)
    n_row, n_col = len(powers(rows)), len(powers(cols))
    used = 2 * len(first) + len(rest)
    last = used + 2 * (n_row + n_col)
    wide = None
    if fits:
        ends = beside.at[:MARGIN, :], beside.at[beside.shape[0] - MARGIN :, :]
        wide = Edges(*ends, *corners, row, rows, sems, last)
    small = [small_reduce(s_acc, s_rx, s_part, s_part_rx, s_all, first, rest, sems, 0)]
    advance_all(small)
    for k in range(tiles):
        a_acc[k * nobs : (k + 1) * nobs, :] = a[:, k * LON : (k + 1) * LON]
    b_acc[...] = b[...]
    large = [all_reduce(a_acc, a_rx, a_all, row, rows, sems, used)]
    other = [all_reduce(b_acc, b_rx, b_all, col, cols, sems, used + 2 * n_row)]
    advance_all(large)
    advance_all(other)
    step = 0
    while small:
        advance_all(small)
        step += 1
        if step % 2 == 0:
            advance_all(other)
        if step % 3 == 0:
            advance_all(large)
    large += other
    if fits:
        wide.start()
    sub = lax.broadcasted_iota(jnp.int32, (nobs, nobs), 0)
    lane = lax.broadcasted_iota(jnp.int32, (nobs, nobs), 1)
    m = s_all[...] + jnp.where(sub == lane, jnp.broadcast_to(r[...], (nobs, nobs)), 0.0)
    inv_out[...] = inverse(0.5 * (m + m.T), lambda: advance_all(large))
    while large:
        advance_all(large)
    reach = STEPS * nobs
    narrow = Edges(
        a_all.at[:reach, :], a_all.at[(tiles - STEPS) * nobs :, :], a_side.at[0], a_side.at[1],
        col, cols, sems, last + 2,
    )
    narrow.start()
    b_out[...] = b_all[...]
    for k in range(tiles):
        c = MARGIN + k * LON
        a_out[:, c : c + LON] = a_all[k * nobs : (k + 1) * nobs, :]
    narrow.finish()
    for k in range(STEPS):
        c = MARGIN + (tiles + k) * LON
        a_out[:, k * LON : (k + 1) * LON] = a_side[0, k * nobs : (k + 1) * nobs, :]
        a_out[:, c : c + LON] = a_side[1, k * nobs : (k + 1) * nobs, :]
    if fits:
        wide.finish()


def small_order(sizes):
    (row, rows), (col, cols) = sizes
    row_powers = powers(rows)
    first = [(row, d) for d in row_powers[:1]] + [(col, d) for d in powers(cols)]
    return first, [(row, d) for d in row_powers[1:]]


def sums(a, b, s, r, beside):
    fits = beside.shape[0] >= MARGIN
    sizes = [(axis, lax.axis_size(axis)) for axis in ("row", "col")]
    first, rest = small_order(sizes)
    copies = 2 * len(first) + len(rest) + 2 * sum(len(powers(n)) for _, n in sizes) + 4
    nobs = s.shape[0]
    part = nobs >> len(first)
    tall = a.shape[0] * a.shape[1] // LON
    vmem = pl.BlockSpec(memory_space=pltpu.VMEM)
    f32 = jnp.float32
    return pl.pallas_call(
        functools.partial(sums_kernel, sizes, fits),
        in_specs=[vmem] * 5,
        out_specs=[vmem] * (3 + 2 * fits),
        out_shape=[
            jax.ShapeDtypeStruct(shape, f32)
            for shape in [(nobs, a.shape[1] + 2 * MARGIN), b.shape, s.shape]
            + [(MARGIN, 2 * MARGIN)] * (2 * fits)
        ],
        scratch_shapes=[
            pltpu.VMEM((tall, LON), f32),
            pltpu.VMEM((tall, LON), f32),
            pltpu.VMEM((tall, LON), f32),
            pltpu.VMEM(b.shape, f32),
            pltpu.VMEM(b.shape, f32),
            pltpu.VMEM(b.shape, f32),
            pltpu.VMEM(s.shape, f32),
            pltpu.VMEM(s.shape, f32),
            pltpu.VMEM((len(rest) + 1, part, nobs), f32),
            pltpu.VMEM((max(len(rest), 1), part, nobs), f32),
            pltpu.VMEM(s.shape, f32),
            pltpu.VMEM((2, STEPS * nobs, LON), f32),
            pltpu.SemaphoreType.DMA((2, copies)),
        ],
        compiler_params=pltpu.CompilerParams(
            collective_id=0, has_side_effects=True, vmem_limit_bytes=VMEM_LIMIT
        ),
        cost_estimate=pl.CostEstimate(
            flops=2 * nobs**3, bytes_accessed=80 * a.size * 4, transcendentals=nobs
        ),
    )(a, b, s, r, beside)


def shards(
    covariance, lon_speed, lat_speed, lon_sign, lat_sign, measurement_site_position, obs_var
):
    rows, cols = covariance.shape
    nobs = obs_var.shape[0]
    row_start = lax.axis_index("row") * rows
    col_start = lax.axis_index("col") * cols
    fields = jnp.stack(
        [lon_speed, lat_speed, lon_sign.astype(jnp.float32), lat_sign.astype(jnp.float32)]
    )
    fields = jnp.pad(fields, ((0, 0), (MARGIN, MARGIN)))
    row_fields = lax.dynamic_slice_in_dim(fields, row_start, rows + 2 * MARGIN, axis=1)
    col_fields = lax.dynamic_slice_in_dim(fields, col_start, cols + 2 * MARGIN, axis=1)
    row_lines = [row_fields[i : i + 1] for i in range(4)]
    col_lines = [col_fields[i : i + 1] for i in range(4)]
    row_coeffs = [
        jnp.broadcast_to(row_fields[i][:, None], (rows + 2 * MARGIN, LON)) for i in range(4)
    ]

    tiles = cols // LON
    beside = jnp.concatenate(halos([covariance], "col", 1), axis=1)
    moved = row_transport(
        covariance, *halos([covariance], "row", 0), row_coeffs, tiles, lambda j: j
    )

    g_row = site_rows(measurement_site_position, row_start, row_lines)
    g_col = site_rows(measurement_site_position, col_start, col_lines)
    dot = functools.partial(
        lax.dot_general, precision=HIGH, preferred_element_type=jnp.float32
    )
    a_part = dot(g_row, covariance, (((1,), (0,)), ((), ())))
    b_part = dot(covariance, g_col, (((1,), (1,)), ((), ())))
    s_part = lax.dot_general(
        a_part, g_col, (((1,), (1,)), ((), ())), precision=HIGHEST, preferred_element_type=jnp.float32
    )
    a_part, b_part, s_part, moved = lax.optimization_barrier((a_part, b_part, s_part, moved))
    a, b, inv, *corners = sums(a_part, b_part, s_part, obs_var.reshape(1, nobs), beside)
    if not corners:
        corners = halos([beside], "row", 0)
    beside = row_transport(beside, *corners, row_coeffs, 2 * STEPS, lambda j: j)
    arrays = [beside, moved]
    pieces = [(0, 0, STEPS), (1, 0, tiles), (0, STEPS, STEPS)]
    b_lo, b_hi = halos([b], "row", 0)
    pht = row_transport(b, b_lo, b_hi, row_coeffs, nobs // LON, lambda j: j)
    wide = cols + 2 * MARGIN
    w_hi, w_lo = pl.pallas_call(
        weights_kernel,
        out_shape=[jax.ShapeDtypeStruct((nobs, cols), jnp.bfloat16)] * 2,
        scratch_shapes=[
            pltpu.VMEM((nobs, cols), jnp.float32),
            pltpu.VMEM((2, nobs, wide), jnp.float32),
        ],
        compiler_params=params(),
    )(a, inv, *col_lines)

    tile = LON
    return pl.pallas_call(
        functools.partial(final_kernel, pieces, len(arrays)),
        grid=(rows // tile,),
        in_specs=[pl.BlockSpec((tile, x.shape[1]), lambda i: (i, 0)) for x in arrays]
        + [
            pl.BlockSpec((tile, nobs), lambda i: (i, 0)),
            pl.BlockSpec((nobs, cols), lambda i: (0, 0)),
            pl.BlockSpec((nobs, cols), lambda i: (0, 0)),
        ]
        + [pl.BlockSpec((1, wide), lambda i: (0, 0))] * 4,
        out_specs=pl.BlockSpec((tile, cols), lambda i: (i, 0)),
        out_shape=jax.ShapeDtypeStruct((rows, cols), jnp.float32),
        scratch_shapes=[pltpu.VMEM((2, tile, wide), jnp.float32)],
        compiler_params=params(),
    )(*arrays, pht, w_hi, w_lo, *col_lines)


def solution(mesh):
    return jax.shard_map(
        shards,
        mesh=mesh,
        in_specs=(P("row", "col"), P(), P(), P(), P(), P(), P()),
        out_specs=P("row", "col"),
        check_vma=False,
    )
```
